512 devices in a mesh: group: 8 (over y_hi, core), shard: 64 (over x, z, y_lo).
Axes of the slice: x: 4, y: 8 (y_hi: 4, y_lo: 2; y = y_hi * 2 + y_lo), z: 8, core: 2. Of those that a mesh axis runs over, the one named last changes fastest.
Arguments:
- learner_inputs: bfloat16 [8, 8192, 8192], P('group', 'shard'), may hold values from -16 to 16
- learner_cotangent: bfloat16 [8, 8192, 4096], P('group', 'shard'), may hold values from -16 to 16
- down_factor: float32 [8192, 64], P('shard'), may hold values from -0.0625 to 0.0625
- up_factor: float32 [4096, 64], P('shard'), may hold values from -0.75 to 0.75
- weight: bfloat16 [8192, 4096], P('shard'), may hold values from -0.0625 to 0.0625
- context: bfloat16 [8, 4, 8, 8192], P('group', None, None, 'shard'), may hold values from -6 to 6
- residual: bfloat16 [8, 4, 8, 4096], P('group'), may hold values from -6 to 6
Outputs:
- new_down: bfloat16 [8192, 64], P('shard')
- new_up: bfloat16 [4096, 64], P('shard')
- decoded: bfloat16 [8, 4, 8, 4096], P('group')
The draws below stay inside these ranges and needn't reach their ends.
All inputs are finite; a program needn't handle non-finite values.
Results may differ from the reference program's by a relative error of at most 0.008.
Values may be sent and summed in bfloat16 or wider, within the bound.
A program may use at most 64 MiB of HBM per device.

```python
import math
import jax
import jax.numpy as jnp

MODEL_WIDTH = 8192
OUTPUT_FEATURES = 4096
ADAPTER_RANK = 64
DROWS = 8
STEPS = 4
LEARNER_TOKENS = 8192
N_GROUP = 8


def strengthened(result, key, source, target, blocks, factor):
    owner, partner = [(jnp.arange(result.shape[dim]) // (result.shape[dim] // blocks)).reshape([-1 if axis == dim else 1 for axis in range(result.ndim)]) for dim in (source, target)]
    chosen = jax.random.permutation(key, blocks)[partner]
    strong = (owner == chosen) | (owner == (partner + blocks // 2) % blocks)
    return jnp.where(strong, factor * result, result)


def block_levels(key, dims, shards, smallest, largest):
    level, own = 1.0, jax.random.fold_in(key, 6)
    for position, shards_of in shards:
        steps = jnp.exp(jax.random.uniform(jax.random.fold_in(own, position), (shards_of,), jnp.float32, smallest / len(shards), largest / len(shards)))
        level = level * jnp.repeat(steps, dims[position] // shards_of).reshape([-1 if axis == position else 1 for axis in range(len(dims))])
    return level


def normal_values(stream_key, extent, scale, most, pieces=(), held_as=jnp.bfloat16):
    drawn = scale * jax.random.normal(stream_key, extent, jnp.float32)
    if pieces:
        drawn = drawn * block_levels(stream_key, extent, pieces, -0.22, 0.18)
    return jnp.clip(drawn, -most, most).astype(held_as)


def heavy_noise(key, dims, deviation, limit, cuts, heavy, kind=jnp.bfloat16):
    array = deviation * jax.random.normal(key, dims, jnp.float32)
    if cuts:
        array = array * block_levels(key, dims, cuts, -0.22, 0.18)
    return jnp.clip(strengthened(array, jax.random.fold_in(key, 3), *heavy), -limit, limit).astype(kind)


def setup_inputs(seed: int = 0) -> dict:
    seeds = jax.random.split(jax.random.key(seed), 8)
    return {
        "learner_inputs": heavy_noise(seeds[0], (N_GROUP, LEARNER_TOKENS, MODEL_WIDTH), 1.0, 16.0, ((0, 8), (1, 64)), (1, 2, 64, 4.0)),
        "learner_cotangent": heavy_noise(seeds[1], (N_GROUP, LEARNER_TOKENS, OUTPUT_FEATURES), 1.0, 16.0, ((0, 8), (1, 64)), (1, 2, 64, 4.0)),
        "down_factor": normal_values(seeds[2], (MODEL_WIDTH, ADAPTER_RANK), MODEL_WIDTH ** -0.5, 0.0625, ((0, 64),), jnp.float32),
        "up_factor": normal_values(seeds[3], (OUTPUT_FEATURES, ADAPTER_RANK), ADAPTER_RANK ** -0.5, 0.75, ((0, 64),), jnp.float32),
        "weight": normal_values(seeds[4], (MODEL_WIDTH, OUTPUT_FEATURES), MODEL_WIDTH ** -0.5, 0.0625, ((0, 64),)),
        "context": normal_values(seeds[5], (N_GROUP, STEPS, DROWS, MODEL_WIDTH), 1.0, 6.0, ((0, 8), (3, 64))),
        "residual": normal_values(seeds[6], (N_GROUP, STEPS, DROWS, OUTPUT_FEATURES), 1.0, 6.0, ((0, 8),)),
    }


adapter_scale = 2.0

def reference(learner_inputs, learner_cotangent, down_factor, up_factor, weight, context, residual):
    current_inputs = learner_inputs[0]
    output_gradient = learner_cotangent[0]
    down_round = down_factor.astype(jnp.bfloat16)
    up_round = up_factor.astype(jnp.bfloat16)
    lowered_rows = jnp.dot(current_inputs, down_round, preferred_element_type=jnp.float32).astype(jnp.bfloat16)
    raised_rows = jnp.dot(output_gradient, up_round, preferred_element_type=jnp.float32).astype(jnp.bfloat16)
    down_gradient = adapter_scale * jnp.dot(current_inputs.T, raised_rows, preferred_element_type=jnp.float32)
    up_gradient = adapter_scale * jnp.dot(output_gradient.T, lowered_rows, preferred_element_type=jnp.float32)
    down_learning_rate = 0.5 * math.sqrt(ADAPTER_RANK) / (adapter_scale * math.sqrt(MODEL_WIDTH * OUTPUT_FEATURES) * math.sqrt(LEARNER_TOKENS))
    up_learning_rate = 0.5 / (adapter_scale * math.sqrt(ADAPTER_RANK) * math.sqrt(LEARNER_TOKENS))
    new_down = (down_factor - down_learning_rate * down_gradient).astype(jnp.bfloat16)
    new_up = (up_factor - up_learning_rate * up_gradient).astype(jnp.bfloat16)
    weight_delta = jnp.dot(new_down, new_up.T, preferred_element_type=jnp.float32)
    combined_weight = (weight.astype(jnp.float32) + adapter_scale * weight_delta).astype(jnp.bfloat16)
    flattened = context.reshape(-1, MODEL_WIDTH)
    projected = jnp.dot(flattened, combined_weight, preferred_element_type=jnp.float32).reshape(residual.shape)
    decoded = (residual.astype(jnp.float32) + projected).astype(jnp.bfloat16)
    return (new_down, new_up, decoded)
```

```python
import functools
import math

import jax
import jax.numpy as jnp
from jax import lax
from jax.experimental import pallas as pl
from jax.experimental.pallas import tpu as pltpu
from jax.sharding import PartitionSpec as P

RANK = 64
SCALE = 2.0
F32 = jnp.float32
BF16 = jnp.bfloat16
NT = (((1,), (1,)), ((), ()))


def torus(shards):
    return {64: (4, 8, 2), 8: (2, 2, 2)}[shards]


def left_half(shape):
    return lax.broadcasted_iota(jnp.int32, shape, 1) < 64


def halves(even, odd):
    keep = left_half(even.shape)
    first = jnp.where(keep, even, pltpu.roll(odd, 64, 1))
    second = jnp.where(keep, pltpu.roll(even, 64, 1), odd)
    return first, second


def kernel(
    sizes, rates,
    x_hbm, c_hbm, down_hbm, up_hbm, w_hbm, ctx_hbm, res_hbm,
    new_ref, dec_ref,
    x_v, c_v, down_v, up_v, w_v, ctx_v, res_v,
    ag, grads, a1, a1s, a2, a2s, a3, b1, b1s, b2, b2s, b3,
    base, p1, p1s, p2, p2s, p3, fresh, tz, tx, ty, txs, tys, outs,
    local_sem, send_sem, recv_sem,
):
    nx, nz, ny, groups = sizes
    group = lax.axis_index("group")
    shard = lax.axis_index("shard")
    y = lax.rem(shard, ny)
    z = lax.rem(shard // ny, nz)
    x = shard // (ny * nz)
    learner = group == 0
    tokens = x_v.shape[0]

    def at(xx, zz, yy):
        return (xx * nz + zz) * ny + yy

    def x_peer(d):
        return lax.rem(x + d, nx)

    def z_peer(d):
        return lax.rem(z + d, nz)

    other = 1 - y

    local = [
        pltpu.make_async_copy(src, dst, local_sem.at[i])
        for i, (src, dst) in enumerate(
            [
                (down_hbm, down_v),
                (up_hbm, up_v),
                (ctx_hbm, ctx_v),
                (w_hbm, w_v),
                (res_hbm.at[:, pl.ds(pl.multiple_of((shard // ny) * 128, 128), 128)], res_v),
                (c_hbm, c_v),
                (x_hbm, x_v),
            ]
        )
    ]
    for copy in local[:5]:
        copy.start()

    @pl.when(learner)
    def _():
        local[5].start()
        local[6].start()

    barrier = pltpu.get_barrier_semaphore()
    peers = (
        [at(x, z_peer(d), y) for d in range(1, nz)]
        + [at(x_peer(d), z, y) for d in range(1, nx)]
        + [at(x, z, other)]
    )
    for peer in peers:
        pl.semaphore_signal(
            barrier, inc=1, device_id={"shard": peer}, device_id_type=pl.DeviceIdType.MESH
        )

    @pl.when(jnp.logical_not(learner))
    def _():
        pl.semaphore_signal(
            barrier, inc=1, device_id={"group": 0}, device_id_type=pl.DeviceIdType.MESH
        )

    pl.semaphore_wait(barrier, len(peers) + jnp.where(learner, groups - 1, 0))

    used = [0]

    def remote(src, dst, peer):
        k = used[0]
        used[0] += 1
        return pltpu.make_async_remote_copy(
            src_ref=src, dst_ref=dst, send_sem=send_sem.at[k], recv_sem=recv_sem.at[k],
            device_id={"shard": peer}, device_id_type=pl.DeviceIdType.MESH,
        )

    def start(copies):
        for copy in copies:
            copy.start()

    def arrive(copies):
        for copy in copies:
            copy.wait_recv()

    gz = [remote(ag.at[y, x, z], ag.at[y, x, z], at(x, z_peer(d), y)) for d in range(1, nz)]
    gax = [
        remote(ag.at[y, x, :, 0:48], ag.at[y, x, :, 0:48], at(x_peer(d), z, y))
        for d in range(1, nx)
    ]
    gay = [remote(ag.at[y, :, :, 0:48], ag.at[y, :, :, 0:48], at(x, z, other))]
    gby = [remote(ag.at[y, x, :, 48:96], ag.at[y, x, :, 48:96], at(x, z, other))]
    gbx = [
        remote(ag.at[:, x, :, 48:96], ag.at[:, x, :, 48:96], at(x_peer(d), z, y))
        for d in range(1, nx)
    ]
    ray = [remote(grads.at[other, :, :, 0:48], a1, at(x, z, other))]
    rax = [remote(a1s.at[x_peer(d)], a2.at[d - 1], at(x_peer(d), z, y)) for d in range(1, nx)]
    raz = [remote(a2s.at[z_peer(d)], a3.at[d - 1], at(x, z_peer(d), y)) for d in range(1, nz)]
    rbx = [
        remote(grads.at[:, x_peer(d), :, 48:96], b1.at[d - 1], at(x_peer(d), z, y))
        for d in range(1, nx)
    ]
    rby = [remote(b1s.at[other], b2, at(x, z, other))]
    rbz = [remote(b2s.at[z_peer(d)], b3.at[d - 1], at(x, z_peer(d), y)) for d in range(1, nz)]
    py = [remote(base.at[other], p1, at(x, z, other))]
    px = [remote(p1s.at[x_peer(d)], p2.at[d - 1], at(x_peer(d), z, y)) for d in range(1, nx)]
    pz = [remote(p2s.at[z_peer(d)], p3.at[d - 1], at(x, z_peer(d), y)) for d in range(1, nz)]
    sz = [remote(tz.at[0], tz.at[d], at(x, z_peer(d), y)) for d in range(1, nz)]
    sx = [remote(tx.at[0], tx.at[d], at(x_peer(d), z, y)) for d in range(1, nx)]
    sy = [remote(ty.at[0], ty.at[1], at(x, z, other))]
    oz = [remote(outs.at[y, x, z], outs.at[y, x, z], at(x, z_peer(d), y)) for d in range(1, nz)]
    ox = [remote(outs.at[y, x], outs.at[y, x], at(x_peer(d), z, y)) for d in range(1, nx)]
    oy = [remote(outs.at[y], outs.at[y], at(x, z, other))]
    k_group = used[0]
    spread = [
        pltpu.make_async_remote_copy(
            src_ref=fresh, dst_ref=fresh, send_sem=send_sem.at[k_group + g - 1],
            recv_sem=recv_sem.at[k_group],
            device_id={"group": g}, device_id_type=pl.DeviceIdType.MESH,
        )
        for g in range(1, groups)
    ]

    def factors():
        down_t = down_v[...].T
        up_t = up_v[...].T
        up_t = jnp.concatenate([up_t, jnp.zeros_like(up_t)], axis=1)
        packed, _ = halves(up_t[0:32], up_t[32:64])
        return down_t, packed

    local[0].wait()
    local[1].wait()

    @pl.when(learner)
    def _():
        down_t, packed = factors()
        ag[y, x, z, 0:64] = down_t.astype(BF16)
        ag[y, x, z, 64:96] = packed.astype(BF16)
        start(gz)

    local[2].wait()
    local[3].wait()

    def project(xx, _):
        for zz in range(nz):
            column = pl.multiple_of((xx * nz + zz) * 128, 128)
            block = jnp.dot(ctx_v[...], w_v[:, pl.ds(column, 128)], preferred_element_type=F32)
            even, odd = halves(block[0:16], block[16:32])
            base[0, xx, zz] = even.astype(BF16)
            base[1, xx, zz] = odd.astype(BF16)
        return 0

    lax.fori_loop(0, nx, project, 0)

    @pl.when(jnp.logical_not(learner))
    def _():
        start(py)

    @pl.when(learner)
    def _():
        arrive(gz)
        start(gax)
        start(gby)
        start(py)
        arrive(gax)
        start(gay)
        arrive(gby)
        start(gbx)

    arrive(py)
    p1s[...] = (base[y].astype(F32) + p1[...].astype(F32)).astype(BF16)
    start(px)
    arrive(px)
    total = p1s[x].astype(F32)
    for d in range(1, nx):
        total = total + p2[d - 1].astype(F32)
    p2s[...] = total.astype(BF16)
    start(pz)

    @pl.when(learner)
    def _():
        local[5].wait()
        arrive(gbx)

        def lift(xx, total):
            for zz in range(nz):
                column = pl.multiple_of((xx * nz + zz) * 128, 128)
                even = ag[0, xx, zz, 64:96].astype(F32)
                odd = ag[1, xx, zz, 64:96].astype(F32)
                top, low = halves(even, odd)
                up_t = jnp.concatenate([top, low], axis=0).astype(BF16)
                total = total + lax.dot_general(
                    up_t, c_v[:, pl.ds(column, 128)], NT, preferred_element_type=F32
                )
            return total

        lifted = lax.fori_loop(0, nx, lift, jnp.zeros((RANK, tokens), F32)).astype(BF16)
        local[6].wait()

        def down_grads(xx, _):
            for zz in range(nz):
                column = pl.multiple_of((xx * nz + zz) * 256, 256)
                block = jnp.dot(lifted, x_v[:, pl.ds(column, 256)], preferred_element_type=F32)
                block = block.astype(BF16)
                grads[0, xx, zz, 0:64] = block[:, 0:128]
                grads[1, xx, zz, 0:64] = block[:, 128:256]
            return 0

        lax.fori_loop(0, nx, down_grads, 0)
        start(ray)
        arrive(gay)

        def lower(xx, total):
            for zz in range(nz):
                column = pl.multiple_of((xx * nz + zz) * 256, 256)
                down_t = jnp.concatenate([ag[0, xx, zz, 0:64], ag[1, xx, zz, 0:64]], axis=1)
                total = total + lax.dot_general(
                    down_t, x_v[:, pl.ds(column, 256)], NT, preferred_element_type=F32
                )
            return total

        lowered = lax.fori_loop(0, nx, lower, jnp.zeros((RANK, tokens), F32)).astype(BF16)

        def up_grads(xx, _):
            for zz in range(nz):
                column = pl.multiple_of((xx * nz + zz) * 128, 128)
                block = jnp.dot(lowered, c_v[:, pl.ds(column, 128)], preferred_element_type=F32)
                even, odd = halves(block[0:32], block[32:64])
                grads[0, xx, zz, 64:96] = even.astype(BF16)
                grads[1, xx, zz, 64:96] = odd.astype(BF16)
            return 0

        lax.fori_loop(0, nx, up_grads, 0)
        start(rbx)
        arrive(ray)
        a1s[...] = (grads[y, :, :, 0:48].astype(F32) + a1[...].astype(F32)).astype(BF16)
        start(rax)
        arrive(rbx)
        total = grads[:, x, :, 48:96].astype(F32)
        for d in range(1, nx):
            total = total + b1[d - 1].astype(F32)
        b1s[...] = total.astype(BF16)
        start(rby)
        arrive(rax)
        total = a1s[x].astype(F32)
        for d in range(1, nx):
            total = total + a2[d - 1].astype(F32)
        a2s[...] = total.astype(BF16)
        start(raz)
        arrive(rby)
        b2s[...] = (b1s[y].astype(F32) + b2[...].astype(F32)).astype(BF16)
        start(rbz)
        arrive(raz)
        down_t, packed = factors()
        total = a2s[z].astype(F32)
        for d in range(1, nz):
            total = total + a3[d - 1].astype(F32)
        fresh[0:48] = (down_t[0:48] - rates[0] * (SCALE * total)).astype(BF16)
        arrive(rbz)
        total = b2s[z].astype(F32)
        for d in range(1, nz):
            total = total + b3[d - 1].astype(F32)
        fresh[48:64] = (down_t[48:64] - rates[0] * (SCALE * total[0:16])).astype(BF16)
        fresh[64:96] = (packed - rates[1] * (SCALE * total[16:48])).astype(BF16)
        start(spread)

    arrive(pz)
    frozen = p2s[z].astype(F32)
    for d in range(1, nz):
        frozen = frozen + p3[d - 1].astype(F32)
    local[4].wait()
    even, odd = halves(res_v[0:16].astype(F32), res_v[16:32].astype(F32))
    frozen = frozen + jnp.where(y == 0, even, odd)

    @pl.when(jnp.logical_not(learner))
    def _():
        spread[0].wait_recv()

    new_down = fresh[0:64]
    nothing = jnp.zeros_like(new_down)
    first = jnp.concatenate([new_down, nothing], axis=0)
    second = jnp.concatenate([nothing, new_down], axis=0)
    tz[0] = lax.dot_general(
        ctx_v[0:16], first, NT, preferred_element_type=F32
    ) + lax.dot_general(ctx_v[16:32], second, NT, preferred_element_type=F32)
    start(sz)
    arrive(sz)
    tx[0] = jnp.sum(tz[...], axis=0)
    start(sx)
    arrive(sx)
    ty[0] = jnp.sum(tx[...], axis=0)
    start(sy)
    arrive(sy)
    lowered_rows = (ty[0] + ty[1]).astype(BF16)
    packed = fresh[64:96].astype(F32)
    turned = pltpu.roll(packed, 64, 1)
    keep = left_half(packed.shape)
    square = jnp.concatenate(
        [
            jnp.where(keep, packed, 0.0),
            jnp.where(keep, turned, 0.0),
            jnp.where(keep, 0.0, turned),
            jnp.where(keep, 0.0, packed),
        ],
        axis=0,
    ).astype(BF16)
    delta = jnp.dot(lowered_rows, square, preferred_element_type=F32)
    outs[y, x, z] = (frozen + SCALE * delta).astype(BF16)
    start(oz)
    new_ref[...] = fresh[...]
    arrive(oz)
    start(ox)
    arrive(ox)
    start(oy)
    arrive(oy)

    def unpack(xx, _):
        for zz in range(nz):
            column = pl.multiple_of((xx * nz + zz) * 128, 128)
            top, low = halves(outs[0, xx, zz].astype(F32), outs[1, xx, zz].astype(F32))
            dec_ref[0:16, pl.ds(column, 128)] = top.astype(BF16)
            dec_ref[16:32, pl.ds(column, 128)] = low.astype(BF16)
        return 0

    lax.fori_loop(0, nx, unpack, 0)

    for copy in py + px + pz + sz + sx + sy + oz + ox + oy:
        copy.wait_send()

    @pl.when(learner)
    def _():
        for copy in gz + gax + gay + gby + gbx + ray + rax + raz + rbx + rby + rbz + spread:
            copy.wait_send()


def per_device(
    sizes, rates,
    learner_inputs, learner_cotangent, down_factor, up_factor, weight, context, residual
):
    nx, nz, ny, groups = sizes
    tokens, width = learner_inputs.shape[1:]
    features = learner_cotangent.shape[2]
    rows = context.shape[1] * context.shape[2]
    copies = 7 * (nz - 1) + 7 * (nx - 1) + 7 + (groups - 1)
    scratch = [
        pltpu.VMEM((tokens, width), BF16),
        pltpu.VMEM((tokens, features), BF16),
        pltpu.VMEM(down_factor.shape, F32),
        pltpu.VMEM(up_factor.shape, F32),
        pltpu.VMEM(weight.shape, BF16),
        pltpu.VMEM((rows, 128), BF16),
        pltpu.VMEM((rows, 128), BF16),
        pltpu.VMEM((ny, nx, nz, 96, 128), BF16),
        pltpu.VMEM((ny, nx, nz, 96, 128), BF16),
        pltpu.VMEM((nx, nz, 48, 128), BF16),
        pltpu.VMEM((nx, nz, 48, 128), BF16),
        pltpu.VMEM((nx - 1, nz, 48, 128), BF16),
        pltpu.VMEM((nz, 48, 128), BF16),
        pltpu.VMEM((nz - 1, 48, 128), BF16),
        pltpu.VMEM((nx - 1, ny, nz, 48, 128), BF16),
        pltpu.VMEM((ny, nz, 48, 128), BF16),
        pltpu.VMEM((nz, 48, 128), BF16),
        pltpu.VMEM((nz, 48, 128), BF16),
        pltpu.VMEM((nz - 1, 48, 128), BF16),
        pltpu.VMEM((ny, nx, nz, 16, 128), BF16),
        pltpu.VMEM((nx, nz, 16, 128), BF16),
        pltpu.VMEM((nx, nz, 16, 128), BF16),
        pltpu.VMEM((nx - 1, nz, 16, 128), BF16),
        pltpu.VMEM((nz, 16, 128), BF16),
        pltpu.VMEM((nz - 1, 16, 128), BF16),
        pltpu.VMEM((96, 128), BF16),
        pltpu.VMEM((nz, 16, 128), F32),
        pltpu.VMEM((nx, 16, 128), F32),
        pltpu.VMEM((ny, 16, 128), F32),
        pltpu.VMEM((16, 128), F32),
        pltpu.VMEM((16, 128), F32),
        pltpu.VMEM((ny, nx, nz, 16, 128), BF16),
        pltpu.SemaphoreType.DMA((7,)),
        pltpu.SemaphoreType.DMA((copies,)),
        pltpu.SemaphoreType.DMA((copies,)),
    ]
    fresh, decoded = pl.pallas_call(
        functools.partial(kernel, sizes, rates),
        out_shape=(
            jax.ShapeDtypeStruct((96, 128), BF16),
            jax.ShapeDtypeStruct((rows, features), BF16),
        ),
        in_specs=[pl.BlockSpec(memory_space=pl.ANY)] * 7,
        out_specs=(pl.BlockSpec(memory_space=pltpu.VMEM),) * 2,
        scratch_shapes=scratch,
        compiler_params=pltpu.CompilerParams(
            collective_id=0, has_side_effects=True, vmem_limit_bytes=40 * 1024 * 1024
        ),
        name="lora_step",
    )(
        learner_inputs[0], learner_cotangent[0], down_factor, up_factor, weight,
        context[0].reshape(rows, -1), residual[0].reshape(rows, features),
    )
    new_down = fresh[0:64].T
    new_up = jnp.concatenate([fresh[64:96, 0:64], fresh[64:96, 64:128]], axis=0).T
    return new_down, new_up, decoded.reshape(residual.shape)


def solution(mesh):
    groups, shards = mesh.shape["group"], mesh.shape["shard"]
    nx, nz, ny = torus(shards)
    placed = (
        P("group", "shard", None),
        P("group", "shard", None),
        P("shard", None),
        P("shard", None),
        P("shard", None),
        P("group", None, None, "shard"),
        P("group", None, None, None),
    )

    def whole(learner_inputs, learner_cotangent, *others):
        tokens, width = learner_inputs.shape[1:]
        features = learner_cotangent.shape[2]
        rates = (
            0.5 * math.sqrt(RANK) / (SCALE * math.sqrt(width * features) * math.sqrt(tokens)),
            0.5 / (SCALE * math.sqrt(RANK) * math.sqrt(tokens)),
        )
        return jax.shard_map(
            functools.partial(per_device, (nx, nz, ny, groups), rates),
            mesh=mesh,
            in_specs=placed,
            out_specs=(P("shard", None), P("shard", None), P("group", None, None, None)),
            check_vma=False,
        )(learner_inputs, learner_cotangent, *others)

    return whole
```

```python
import functools
import math

import jax
import jax.numpy as jnp
from jax import lax
from jax.experimental import pallas as pl
from jax.experimental.pallas import tpu as pltpu
from jax.sharding import PartitionSpec as P

RANK = 64
SCALE = 2.0
F32 = jnp.float32
BF16 = jnp.bfloat16
NT = (((1,), (1,)), ((), ()))


def torus(shards):
    return {64: (4, 8, 2), 8: (2, 2, 2)}[shards]


def left_half(shape):
    return lax.broadcasted_iota(jnp.int32, shape, 1) < 64


def halves(even, odd):
    keep = left_half(even.shape)
    first = jnp.where(keep, even, pltpu.roll(odd, 64, 1))
    second = jnp.where(keep, pltpu.roll(even, 64, 1), odd)
    return first, second


def kernel(
    sizes, rates,
    x_hbm, c_hbm, down_hbm, up_hbm, w_hbm, ctx_hbm, res_hbm,
    new_ref, dec_ref,
    x_v, c_v, down_v, up_v, w_v, ctx_v, res_v,
    up_all, down_all, up_flat, down_flat,
    gd, rd, sd, qd, gu, ru, su, qu,
    base, rb, sb, qb, fresh, tz, txy, outs,
    local_sem, send_sem, recv_sem,
):
    nx, nz, ny, groups = sizes
    group = lax.axis_index("group")
    shard = lax.axis_index("shard")
    y = lax.rem(shard, ny)
    z = lax.rem(shard // ny, nz)
    x = shard // (ny * nz)
    other = 1 - y
    learner = group == 0

    def at(xx, zz, yy):
        return (xx * nz + zz) * ny + yy

    def x_to(d):
        return lax.rem(x + d, nx)

    def z_to(d):
        return lax.rem(z + d, nz)

    def y_to(d):
        return lax.rem(y + d, ny)

    def hops(d, n):
        return min(d, n - d)

    line = sorted(range(1, nz), key=lambda d: -hops(d, nz))
    rows = sorted(range(nx), key=lambda d: -hops(d, nx))
    plane = [(dx, dy) for dx in rows for dy in (1, 0) if (dx, dy) != (0, 0)]

    local = [
        pltpu.make_async_copy(src, dst, local_sem.at[i])
        for i, (src, dst) in enumerate(
            [
                (up_hbm, up_v),
                (down_hbm, down_v),
                (ctx_hbm, ctx_v),
                (w_hbm, w_v),
                (res_hbm.at[:, pl.ds(pl.multiple_of((shard // ny) * 128, 128), 128)], res_v),
                (c_hbm, c_v),
                (x_hbm, x_v),
            ]
        )
    ]
    for copy in local[:5]:
        copy.start()

    @pl.when(learner)
    def _():
        local[5].start()
        local[6].start()

    barrier = pltpu.get_barrier_semaphore()
    peers = [at(x, z_to(d), y) for d in line] + [at(x_to(dx), z, y_to(dy)) for dx, dy in plane]
    for peer in peers:
        pl.semaphore_signal(
            barrier, inc=1, device_id={"shard": peer}, device_id_type=pl.DeviceIdType.MESH
        )

    @pl.when(jnp.logical_not(learner))
    def _():
        pl.semaphore_signal(
            barrier, inc=1, device_id={"group": 0}, device_id_type=pl.DeviceIdType.MESH
        )

    used = [0]

    def remote(src, dst, peer):
        k = used[0]
        used[0] += 1
        return pltpu.make_async_remote_copy(
            src_ref=src, dst_ref=dst, send_sem=send_sem.at[k], recv_sem=recv_sem.at[k],
            device_id={"shard": peer}, device_id_type=pl.DeviceIdType.MESH,
        )

    def along(ref_of, dst_of):
        return [remote(ref_of(z_to(d)), dst_of(i, d), at(x, z_to(d), y)) for i, d in enumerate(line)]

    def across(ref_of, dst_of):
        return [
            remote(ref_of(x_to(dx), y_to(dy)), dst_of(i), at(x_to(dx), z, y_to(dy)))
            for i, (dx, dy) in enumerate(plane)
        ]

    def start(copies, started):
        for copy in copies:
            copy.start()
        started.extend(copies)

    def arrive(copies):
        for copy in copies:
            copy.wait_recv()

    def sent(started):
        for copy in started:
            copy.wait_send()

    learnt, decoded = [], []

    up_z = along(lambda zz: up_all.at[y, x, z], lambda i, d: up_all.at[y, x, z])
    up_xy = [
        across(lambda xx, yy: up_all.at[y, x, zz], lambda i: up_all.at[y, x, zz])
        for zz in [z] + [lax.rem(z + nz - d, nz) for d in line[::-1]]
    ]
    down_z = along(lambda zz: down_all.at[y, x, z], lambda i, d: down_all.at[y, x, z])
    down_xy = across(lambda xx, yy: down_all.at[y, x], lambda i: down_all.at[y, x])
    gd_xy = across(lambda xx, yy: gd.at[yy, xx], lambda i: rd.at[i])
    gd_z = along(lambda zz: sd.at[zz], lambda i, d: qd.at[i])
    gu_xy = across(lambda xx, yy: gu.at[yy, xx], lambda i: ru.at[i])
    gu_z = along(lambda zz: su.at[zz], lambda i, d: qu.at[i])
    base_xy = across(lambda xx, yy: base.at[yy, xx], lambda i: rb.at[i])
    base_z = along(lambda zz: sb.at[zz], lambda i, d: qb.at[i])
    low_z = along(lambda zz: tz.at[0], lambda i, d: tz.at[i + 1])
    low_xy = across(lambda xx, yy: txy.at[0], lambda i: txy.at[i + 1])
    out_z = along(lambda zz: outs.at[y, x, z], lambda i, d: outs.at[y, x, z])
    out_xy = across(lambda xx, yy: outs.at[y, x], lambda i: outs.at[y, x])

    def spread(part, k):
        order = [g for hi in (2, 1, 3, 0) for g in (2 * hi, 2 * hi + 1) if 0 < g < groups]
        return [
            pltpu.make_async_remote_copy(
                src_ref=part, dst_ref=part, send_sem=send_sem.at[k + i], recv_sem=recv_sem.at[k],
                device_id={"group": g}, device_id_type=pl.DeviceIdType.MESH,
            )
            for i, g in enumerate(order)
        ]

    down_spread = spread(fresh.at[0:64], used[0])
    up_spread = spread(fresh.at[64:96], used[0] + groups - 1)

    def summed(own, others, index=()):
        total = own.astype(F32)
        for i in range(others.shape[0]):
            total = total + others[(i, *index)].astype(F32)
        return total

    def packed_up():
        up_t = up_v[...].T
        up_t = jnp.concatenate([up_t, jnp.zeros_like(up_t)], axis=1)
        return halves(up_t[0:32], up_t[32:64])[0]

    def project(xx, _):
        for zz in range(nz):
            column = pl.multiple_of((xx * nz + zz) * 128, 128)
            block = jnp.dot(ctx_v[...], w_v[:, pl.ds(column, 128)], preferred_element_type=F32)
            even, odd = halves(block[0:16], block[16:32])
            base[0, xx, zz] = even.astype(BF16)
            base[1, xx, zz] = odd.astype(BF16)
        return 0

    def base_lines():
        arrive(base_xy)
        for d, copy in zip(line, base_z):
            zz = z_to(d)
            sb[zz] = summed(base[y, x, zz], rb, (zz,)).astype(BF16)
            copy.start()
        sb[z] = summed(base[y, x, z], rb, (z,)).astype(BF16)

    local[0].wait()
    packed = packed_up()
    pl.semaphore_wait(barrier, len(peers) + jnp.where(learner, groups - 1, 0))

    @pl.when(learner)
    def _():
        up_all[y, x, z] = packed.astype(BF16)
        start(up_z, learnt)
        start(up_xy[0], learnt)
        local[1].wait()
        down_all[y, x, z] = down_v[...].astype(BF16)
        for copy, onward in zip(up_z[::-1], up_xy[1:]):
            arrive([copy])
            start(onward, learnt)
        start(down_z, learnt)

    @pl.when(jnp.logical_not(learner))
    def _():
        local[1].wait()

    local[2].wait()
    local[3].wait()
    lax.fori_loop(0, nx, project, 0)

    @pl.when(jnp.logical_not(learner))
    def _():
        start(base_xy, [])
        base_lines()

    @pl.when(learner)
    def _():
        arrive(down_z)
        start(down_xy, learnt)
        local[5].wait()
        for copies in up_xy:
            arrive(copies)

        def unpack_up(xx, _):
            for zz in range(nz):
                column = pl.multiple_of((xx * nz + zz) * 128, 128)
                top, low = halves(
                    up_all[0, xx, zz].astype(F32), up_all[1, xx, zz].astype(F32)
                )
                up_flat[:, pl.ds(column, 128)] = jnp.concatenate([top, low], axis=0).astype(BF16)
            return 0

        lax.fori_loop(0, nx, unpack_up, 0)
        lifted = lax.dot_general(
            up_flat[...], c_v[...], NT, preferred_element_type=F32
        ).astype(BF16)
        local[6].wait()
        for dx in rows:
            xx = x_to(dx)
            for zz in range(nz):
                column = pl.multiple_of((xx * nz + zz) * 256, 256)
                block = jnp.dot(lifted, x_v[:, pl.ds(column, 256)], preferred_element_type=F32)
                block = block.astype(BF16)
                gd[0, xx, zz] = block[:, 0:128]
                gd[1, xx, zz] = block[:, 128:256]
            start([c for c, p in zip(gd_xy, plane) if p[0] == dx], learnt)
        start(base_xy, [])
        arrive(down_xy)

        def flatten(xx, _):
            for zz in range(nz):
                column = pl.multiple_of((xx * nz + zz) * 256, 256)
                down_flat[:, pl.ds(column, 256)] = jnp.concatenate(
                    [down_all[0, xx, zz], down_all[1, xx, zz]], axis=1
                )
            return 0

        lax.fori_loop(0, nx, flatten, 0)
        lowered = lax.dot_general(
            down_flat[...], x_v[...], NT, preferred_element_type=F32
        ).astype(BF16)
        for dx in rows:
            xx = x_to(dx)
            for zz in range(nz):
                column = pl.multiple_of((xx * nz + zz) * 128, 128)
                block = jnp.dot(lowered, c_v[:, pl.ds(column, 128)], preferred_element_type=F32)
                even, odd = halves(block[0:32], block[32:64])
                gu[0, xx, zz] = even.astype(BF16)
                gu[1, xx, zz] = odd.astype(BF16)
            start([c for c, p in zip(gu_xy, plane) if p[0] == dx], learnt)
        arrive(gd_xy)
        for d, copy in zip(line, gd_z):
            zz = z_to(d)
            sd[zz] = summed(gd[y, x, zz], rd, (zz,)).astype(BF16)
            start([copy], learnt)
        sd[z] = summed(gd[y, x, z], rd, (z,)).astype(BF16)
        base_lines()
        arrive(gd_z)
        total = summed(sd[z], qd)
        fresh[0:64] = (down_v[...] - rates[0] * (SCALE * total)).astype(BF16)
        start(down_spread, learnt)

    decoded.extend(base_xy + base_z)

    @pl.when(jnp.logical_not(learner))
    def _():
        down_spread[0].wait_recv()

    new_down = fresh[0:64]
    nothing = jnp.zeros_like(new_down)
    first = jnp.concatenate([new_down, nothing], axis=0)
    second = jnp.concatenate([nothing, new_down], axis=0)
    tz[0] = lax.dot_general(
        ctx_v[0:16], first, NT, preferred_element_type=F32
    ) + lax.dot_general(ctx_v[16:32], second, NT, preferred_element_type=F32)
    start(low_z, decoded)

    @pl.when(learner)
    def _():
        arrive(gu_xy)
        for d, copy in zip(line, gu_z):
            zz = z_to(d)
            su[zz] = summed(gu[y, x, zz], ru, (zz,)).astype(BF16)
            start([copy], learnt)
        su[z] = summed(gu[y, x, z], ru, (z,)).astype(BF16)

    arrive(base_z)
    local[4].wait()
    even, odd = halves(res_v[0:16].astype(F32), res_v[16:32].astype(F32))
    frozen = summed(sb[z], qb) + jnp.where(y == 0, even, odd)
    arrive(low_z)
    txy[0] = jnp.sum(tz[...], axis=0)
    start(low_xy, decoded)

    @pl.when(learner)
    def _():
        arrive(gu_z)
        fresh[64:96] = (packed - rates[1] * (SCALE * summed(su[z], qu))).astype(BF16)
        start(up_spread, learnt)

    @pl.when(jnp.logical_not(learner))
    def _():
        up_spread[0].wait_recv()

    new_up = fresh[64:96].astype(F32)
    turned = pltpu.roll(new_up, 64, 1)
    keep = left_half(new_up.shape)
    square = jnp.concatenate(
        [
            jnp.where(keep, new_up, 0.0),
            jnp.where(keep, turned, 0.0),
            jnp.where(keep, 0.0, turned),
            jnp.where(keep, 0.0, new_up),
        ],
        axis=0,
    ).astype(BF16)
    arrive(low_xy)
    lowered_rows = jnp.sum(txy[...], axis=0).astype(BF16)
    delta = jnp.dot(lowered_rows, square, preferred_element_type=F32)
    outs[y, x, z] = (frozen + SCALE * delta).astype(BF16)
    start(out_z, decoded)
    new_ref[...] = fresh[...]
    arrive(out_z)
    start(out_xy, decoded)
    arrive(out_xy)

    def unpack(xx, _):
        for zz in range(nz):
            column = pl.multiple_of((xx * nz + zz) * 128, 128)
            top, low = halves(outs[0, xx, zz].astype(F32), outs[1, xx, zz].astype(F32))
            dec_ref[0:16, pl.ds(column, 128)] = top.astype(BF16)
            dec_ref[16:32, pl.ds(column, 128)] = low.astype(BF16)
        return 0

    lax.fori_loop(0, nx, unpack, 0)

    sent(decoded)

    @pl.when(learner)
    def _():
        sent(learnt)


def per_device(
    sizes, rates,
    learner_inputs, learner_cotangent, down_factor, up_factor, weight, context, residual
):
    nx, nz, ny, groups = sizes
    tokens, width = learner_inputs.shape[1:]
    features = learner_cotangent.shape[2]
    rows = context.shape[1] * context.shape[2]
    xy = nx * ny - 1
    copies = 7 * (nz - 1) + (6 + nz) * xy + 2 * (groups - 1)
    blocks = (ny, nx, nz)
    scratch = [
        pltpu.VMEM((tokens, width), BF16),
        pltpu.VMEM((tokens, features), BF16),
        pltpu.VMEM(down_factor.shape[::-1], F32),
        pltpu.VMEM(up_factor.shape, F32),
        pltpu.VMEM(weight.shape, BF16),
        pltpu.VMEM((rows, 128), BF16),
        pltpu.VMEM((rows, 128), BF16),
        pltpu.VMEM((*blocks, 32, 128), BF16),
        pltpu.VMEM((*blocks, 64, 128), BF16),
        pltpu.VMEM((RANK, features), BF16),
        pltpu.VMEM((RANK, width), BF16),
    ]
    for height in (64, 32, 16):
        scratch += [
            pltpu.VMEM((*blocks, height, 128), BF16),
            pltpu.VMEM((xy, nz, height, 128), BF16),
            pltpu.VMEM((nz, height, 128), BF16),
            pltpu.VMEM((nz - 1, height, 128), BF16),
        ]
    scratch += [
        pltpu.VMEM((96, 128), BF16),
        pltpu.VMEM((nz, 16, 128), F32),
        pltpu.VMEM((xy + 1, 16, 128), F32),
        pltpu.VMEM((*blocks, 16, 128), BF16),
        pltpu.SemaphoreType.DMA((7,)),
        pltpu.SemaphoreType.DMA((copies,)),
        pltpu.SemaphoreType.DMA((copies,)),
    ]
    fresh, decoded = pl.pallas_call(
        functools.partial(kernel, sizes, rates),
        out_shape=(
            jax.ShapeDtypeStruct((96, 128), BF16),
            jax.ShapeDtypeStruct((rows, features), BF16),
        ),
        in_specs=[pl.BlockSpec(memory_space=pltpu.HBM)] * 7,
        out_specs=(pl.BlockSpec(memory_space=pltpu.VMEM),) * 2,
        scratch_shapes=scratch,
        compiler_params=pltpu.CompilerParams(
            collective_id=0, has_side_effects=True, vmem_limit_bytes=63 * 1024 * 1024
        ),
        name="lora_step",
    )(
        learner_inputs[0], learner_cotangent[0], down_factor.T, up_factor, weight,
        context[0].reshape(rows, -1), residual[0].reshape(rows, features),
    )
    new_down = fresh[0:64].T
    new_up = jnp.concatenate([fresh[64:96, 0:64], fresh[64:96, 64:128]], axis=0).T
    return new_down, new_up, decoded.reshape(residual.shape)


def solution(mesh):
    groups, shards = mesh.shape["group"], mesh.shape["shard"]
    nx, nz, ny = torus(shards)
    placed = (
        P("group", "shard", None),
        P("group", "shard", None),
        P("shard", None),
        P("shard", None),
        P("shard", None),
        P("group", None, None, "shard"),
        P("group", None, None, None),
    )

    def whole(learner_inputs, learner_cotangent, *others):
        tokens, width = learner_inputs.shape[1:]
        features = learner_cotangent.shape[2]
        rates = (
            0.5 * math.sqrt(RANK) / (SCALE * math.sqrt(width * features) * math.sqrt(tokens)),
            0.5 / (SCALE * math.sqrt(RANK) * math.sqrt(tokens)),
        )
        return jax.shard_map(
            functools.partial(per_device, (nx, nz, ny, groups), rates),
            mesh=mesh,
            in_specs=placed,
            out_specs=(P("shard", None), P("shard", None), P("group", None, None, None)),
            check_vma=False,
        )(learner_inputs, learner_cotangent, *others)

    return whole
```

```python
import functools
import math

import jax
import jax.numpy as jnp
from jax import lax
from jax.experimental import pallas as pl
from jax.experimental.pallas import tpu as pltpu
from jax.sharding import PartitionSpec as P

RANK = 64
SCALE = 2.0
F32 = jnp.float32
BF16 = jnp.bfloat16
NT = (((1,), (1,)), ((), ()))


def torus(shards):
    return {64: (4, 8, 2), 8: (2, 2, 2)}[shards]


def left_half(shape):
    return lax.broadcasted_iota(jnp.int32, shape, 1) < 64


def halves(even, odd):
    keep = left_half(even.shape)
    first = jnp.where(keep, even, pltpu.roll(odd, 64, 1))
    second = jnp.where(keep, pltpu.roll(even, 64, 1), odd)
    return first, second


def kernel(
    sizes, rates,
    x_hbm, c_hbm, down_hbm, up_hbm, w_hbm, ctx_hbm, res_hbm,
    new_ref, out_hbm,
    x_v, c_v, down_v, up_v, w_v, ctx_v, res_v,
    up_all, down_all, up_flat, down_flat,
    gd, rd, sd, qd, gu, ru, su, qu,
    base, rb, sb, qb, fresh, tz, txy, outs,
    local_sem, send_sem, recv_sem,
):
    nx, nz, ny, groups = sizes
    group = lax.axis_index("group")
    shard = lax.axis_index("shard")
    y = lax.rem(shard, ny)
    z = lax.rem(shard // ny, nz)
    x = shard // (ny * nz)
    other = 1 - y
    learner = group == 0
    helper_group = jnp.where(other == 1, groups - 2, 2)
    helper = group == jnp.where(y == 1, groups - 2, 2)

    def at(xx, zz, yy):
        return (xx * nz + zz) * ny + yy

    def x_to(d):
        return lax.rem(x + d, nx)

    def z_to(d):
        return lax.rem(z + d, nz)

    def y_to(d):
        return lax.rem(y + d, ny)

    def hops(d, n):
        return min(d, n - d)

    line = sorted(range(1, nz), key=lambda d: -hops(d, nz))
    rows = sorted(range(nx), key=lambda d: -hops(d, nx))
    plane = [(dx, dy) for dx in rows for dy in (1, 0) if (dx, dy) != (0, 0)]

    local = [
        pltpu.make_async_copy(src, dst, local_sem.at[i])
        for i, (src, dst) in enumerate(
            [
                (up_hbm, up_v),
                (down_hbm, down_v),
                (ctx_hbm, ctx_v),
                (w_hbm, w_v),
                (res_hbm.at[:, pl.ds(pl.multiple_of((shard // ny) * 128, 128), 128)], res_v),
                (c_hbm, c_v),
                (x_hbm, x_v),
            ]
        )
    ]
    for copy in local[:5]:
        copy.start()

    @pl.when(learner)
    def _():
        local[5].start()
        local[6].start()

    barrier = pltpu.get_barrier_semaphore()
    peers = [at(x, z_to(d), y) for d in line] + [at(x_to(dx), z, y_to(dy)) for dx, dy in plane]
    for peer in peers:
        pl.semaphore_signal(
            barrier, inc=1, device_id={"shard": peer}, device_id_type=pl.DeviceIdType.MESH
        )

    @pl.when(jnp.logical_not(learner))
    def _():
        pl.semaphore_signal(
            barrier, inc=1, device_id={"group": 0}, device_id_type=pl.DeviceIdType.MESH
        )

    @pl.when(learner)
    def _():
        for d in range(nx):
            pl.semaphore_signal(
                barrier, inc=1, device_id={"group": helper_group, "shard": at(x_to(d), z, other)},
                device_id_type=pl.DeviceIdType.MESH,
            )

    used = [0]

    def remote(src, dst, peer):
        k = used[0]
        used[0] += 1
        return pltpu.make_async_remote_copy(
            src_ref=src, dst_ref=dst, send_sem=send_sem.at[k], recv_sem=recv_sem.at[k],
            device_id={"shard": peer}, device_id_type=pl.DeviceIdType.MESH,
        )

    def along(ref_of, dst_of):
        return [remote(ref_of(z_to(d)), dst_of(i, d), at(x, z_to(d), y)) for i, d in enumerate(line)]

    def across(ref_of, dst_of):
        return [
            remote(ref_of(x_to(dx), y_to(dy)), dst_of(i), at(x_to(dx), z, y_to(dy)))
            for i, (dx, dy) in enumerate(plane)
        ]

    def beside(ref):
        return [remote(ref, ref, at(x_to(d), z, y)) for d in rows if d]

    def helped(ref):
        copies = []
        for d in rows:
            k = used[0]
            used[0] += 1
            copies.append(
                pltpu.make_async_remote_copy(
                    src_ref=ref, dst_ref=ref, send_sem=send_sem.at[k], recv_sem=recv_sem.at[k],
                    device_id={"group": 0, "shard": at(x_to(d), z, other)},
                    device_id_type=pl.DeviceIdType.MESH,
                )
            )
        return copies

    def start(copies, started):
        for copy in copies:
            copy.start()
        started.extend(copies)

    def arrive(copies):
        for copy in copies:
            copy.wait_recv()

    def sent(started):
        for copy in started:
            copy.wait_send()

    learnt, lent, decoded = [], [], []

    up_z = along(lambda zz: up_all.at[y, x, z], lambda i, d: up_all.at[y, x, z])
    down_z = along(lambda zz: down_all.at[y, x, z], lambda i, d: down_all.at[y, x, z])
    up_x = beside(up_all.at[y, x])
    up_y = helped(up_all.at[y, x])
    down_x = beside(down_all.at[y, x])
    down_y = helped(down_all.at[y, x])
    gd_xy = across(lambda xx, yy: gd.at[yy, xx], lambda i: rd.at[i])
    gd_z = along(lambda zz: sd.at[zz], lambda i, d: qd.at[i])
    gu_xy = across(lambda xx, yy: gu.at[yy, xx], lambda i: ru.at[i])
    gu_z = along(lambda zz: su.at[zz], lambda i, d: qu.at[i])
    base_xy = across(lambda xx, yy: base.at[yy, xx], lambda i: rb.at[i])
    base_z = along(lambda zz: sb.at[zz], lambda i, d: qb.at[i])
    low_z = along(lambda zz: tz.at[0], lambda i, d: tz.at[i + 1])
    low_xy = across(lambda xx, yy: txy.at[0], lambda i: txy.at[i + 1])
    out_z = along(lambda zz: outs.at[y, x, z], lambda i, d: outs.at[y, x, z])
    out_xy = across(lambda xx, yy: outs.at[y, x], lambda i: out_hbm.at[y, x])
    out_own = pltpu.make_async_copy(outs.at[y, x], out_hbm.at[y, x], local_sem.at[7])

    def spread(part, k):
        order = [g for hi in (2, 1, 3, 0) for g in (2 * hi, 2 * hi + 1) if 0 < g < groups]
        return [
            pltpu.make_async_remote_copy(
                src_ref=part, dst_ref=part, send_sem=send_sem.at[k + i], recv_sem=recv_sem.at[k],
                device_id={"group": g}, device_id_type=pl.DeviceIdType.MESH,
            )
            for i, g in enumerate(order)
        ]

    down_spread = spread(fresh.at[0:64], used[0])
    up_spread = spread(fresh.at[64:96], used[0] + groups - 1)

    def summed(own, others, index=()):
        total = own.astype(F32)
        for i in range(others.shape[0]):
            total = total + others[(i, *index)].astype(F32)
        return total

    def packed_up():
        up_t = up_v[...].T
        up_t = jnp.concatenate([up_t, jnp.zeros_like(up_t)], axis=1)
        return halves(up_t[0:32], up_t[32:64])[0]

    def project(xx, _):
        for zz in range(nz):
            column = pl.multiple_of((xx * nz + zz) * 128, 128)
            block = jnp.dot(ctx_v[...], w_v[:, pl.ds(column, 128)], preferred_element_type=F32)
            even, odd = halves(block[0:16], block[16:32])
            base[0, xx, zz] = even.astype(BF16)
            base[1, xx, zz] = odd.astype(BF16)
        return 0

    def base_lines():
        arrive(base_xy)
        for d, copy in zip(line, base_z):
            zz = z_to(d)
            sb[zz] = summed(base[y, x, zz], rb, (zz,)).astype(BF16)
            copy.start()
        sb[z] = summed(base[y, x, z], rb, (z,)).astype(BF16)

    local[0].wait()
    packed = packed_up()
    pl.semaphore_wait(
        barrier,
        len(peers) + jnp.where(learner, groups - 1, 0) + jnp.where(helper, nx, 0),
    )

    local[1].wait()

    @pl.when(jnp.logical_or(learner, helper))
    def _():
        up_all[y, x, z] = packed.astype(BF16)
        for copy in up_z:
            copy.start()
        down_all[y, x, z] = down_v[...].astype(BF16)
        for copy in down_z:
            copy.start()
        arrive(up_z)

        @pl.when(learner)
        def _():
            start(up_x, learnt)

        @pl.when(helper)
        def _():
            start(up_y, lent)

        arrive(down_z)

        @pl.when(learner)
        def _():
            start(down_x, learnt)

        @pl.when(helper)
        def _():
            start(down_y, lent)

    learnt.extend(up_z + down_z)
    lent.extend(up_z + down_z)
    local[2].wait()
    local[3].wait()
    lax.fori_loop(0, nx, project, 0)

    @pl.when(jnp.logical_not(learner))
    def _():
        start(base_xy, [])
        base_lines()

    @pl.when(learner)
    def _():
        local[5].wait()
        arrive(up_x)
        arrive(up_y)

        def unpack_up(xx, _):
            for zz in range(nz):
                column = pl.multiple_of((xx * nz + zz) * 128, 128)
                top, low = halves(
                    up_all[0, xx, zz].astype(F32), up_all[1, xx, zz].astype(F32)
                )
                up_flat[:, pl.ds(column, 128)] = jnp.concatenate([top, low], axis=0).astype(BF16)
            return 0

        lax.fori_loop(0, nx, unpack_up, 0)
        lifted = lax.dot_general(
            up_flat[...], c_v[...], NT, preferred_element_type=F32
        ).astype(BF16)
        local[6].wait()
        for dx in rows:
            xx = x_to(dx)
            for zz in range(nz):
                column = pl.multiple_of((xx * nz + zz) * 256, 256)
                block = jnp.dot(lifted, x_v[:, pl.ds(column, 256)], preferred_element_type=F32)
                block = block.astype(BF16)
                gd[0, xx, zz] = block[:, 0:128]
                gd[1, xx, zz] = block[:, 128:256]
            start([c for c, p in zip(gd_xy, plane) if p[0] == dx], learnt)
        start(base_xy, [])
        arrive(down_x)
        arrive(down_y)

        def flatten(xx, _):
            for zz in range(nz):
                column = pl.multiple_of((xx * nz + zz) * 256, 256)
                down_flat[:, pl.ds(column, 256)] = jnp.concatenate(
                    [down_all[0, xx, zz], down_all[1, xx, zz]], axis=1
                )
            return 0

        lax.fori_loop(0, nx, flatten, 0)
        lowered = lax.dot_general(
            down_flat[...], x_v[...], NT, preferred_element_type=F32
        ).astype(BF16)
        for dx in rows:
            xx = x_to(dx)
            for zz in range(nz):
                column = pl.multiple_of((xx * nz + zz) * 128, 128)
                block = jnp.dot(lowered, c_v[:, pl.ds(column, 128)], preferred_element_type=F32)
                even, odd = halves(block[0:32], block[32:64])
                gu[0, xx, zz] = even.astype(BF16)
                gu[1, xx, zz] = odd.astype(BF16)
            start([c for c, p in zip(gu_xy, plane) if p[0] == dx], learnt)
        arrive(gd_xy)
        for d, copy in zip(line, gd_z):
            zz = z_to(d)
            sd[zz] = summed(gd[y, x, zz], rd, (zz,)).astype(BF16)
            start([copy], learnt)
        sd[z] = summed(gd[y, x, z], rd, (z,)).astype(BF16)
        base_lines()
        arrive(gd_z)
        total = summed(sd[z], qd)
        fresh[0:64] = (down_v[...] - rates[0] * (SCALE * total)).astype(BF16)
        start(down_spread, learnt)

    decoded.extend(base_xy + base_z)

    @pl.when(jnp.logical_not(learner))
    def _():
        down_spread[0].wait_recv()

    new_down = fresh[0:64]
    nothing = jnp.zeros_like(new_down)
    first = jnp.concatenate([new_down, nothing], axis=0)
    second = jnp.concatenate([nothing, new_down], axis=0)
    tz[0] = lax.dot_general(
        ctx_v[0:16], first, NT, preferred_element_type=F32
    ) + lax.dot_general(ctx_v[16:32], second, NT, preferred_element_type=F32)
    start(low_z, decoded)

    @pl.when(learner)
    def _():
        arrive(gu_xy)
        for d, copy in zip(line, gu_z):
            zz = z_to(d)
            su[zz] = summed(gu[y, x, zz], ru, (zz,)).astype(BF16)
            start([copy], learnt)
        su[z] = summed(gu[y, x, z], ru, (z,)).astype(BF16)

    arrive(base_z)
    local[4].wait()
    even, odd = halves(res_v[0:16].astype(F32), res_v[16:32].astype(F32))
    frozen = summed(sb[z], qb) + jnp.where(y == 0, even, odd)
    arrive(low_z)
    txy[0] = jnp.sum(tz[...], axis=0)
    start(low_xy, decoded)

    @pl.when(learner)
    def _():
        arrive(gu_z)
        fresh[64:96] = (packed - rates[1] * (SCALE * summed(su[z], qu))).astype(BF16)
        start(up_spread, learnt)

    @pl.when(jnp.logical_not(learner))
    def _():
        up_spread[0].wait_recv()

    new_up = fresh[64:96].astype(F32)
    turned = pltpu.roll(new_up, 64, 1)
    keep = left_half(new_up.shape)
    square = jnp.concatenate(
        [
            jnp.where(keep, new_up, 0.0),
            jnp.where(keep, turned, 0.0),
            jnp.where(keep, 0.0, turned),
            jnp.where(keep, 0.0, new_up),
        ],
        axis=0,
    ).astype(BF16)
    arrive(low_xy)
    lowered_rows = jnp.sum(txy[...], axis=0).astype(BF16)
    delta = jnp.dot(lowered_rows, square, preferred_element_type=F32)
    outs[y, x, z] = (frozen + SCALE * delta).astype(BF16)
    start(out_z, decoded)
    new_ref[...] = fresh[...]
    arrive(out_z)
    start(out_xy, decoded)
    out_own.start()
    arrive(out_xy)

    out_own.wait()
    sent(decoded)

    @pl.when(learner)
    def _():
        sent(learnt)

    @pl.when(helper)
    def _():
        sent(lent)


def finish(fresh_ref, outs_ref, down_ref, up_ref, dec_ref):
    ny, nx, nz = outs_ref.shape[:3]
    down_ref[...] = fresh_ref[0:64]
    packed = fresh_ref[64:96].astype(F32)
    up_t = jnp.concatenate([packed, pltpu.roll(packed, 64, 1)], axis=0)
    up_ref[...] = up_t.T[0:64].astype(BF16)
    for xx in range(nx):
        for zz in range(nz):
            column = (xx * nz + zz) * 128
            top, low = halves(outs_ref[0, xx, zz].astype(F32), outs_ref[1, xx, zz].astype(F32))
            dec_ref[0:16, column : column + 128] = top.astype(BF16)
            dec_ref[16:32, column : column + 128] = low.astype(BF16)


def per_device(
    sizes, rates,
    learner_inputs, learner_cotangent, down_factor, up_factor, weight, context, residual
):
    nx, nz, ny, groups = sizes
    tokens, width = learner_inputs.shape[1:]
    features = learner_cotangent.shape[2]
    rows = context.shape[1] * context.shape[2]
    xy = nx * ny - 1
    copies = 7 * (nz - 1) + 5 * xy + 2 * (2 * nx - 1) + 2 * (groups - 1)
    blocks = (ny, nx, nz)
    scratch = [
        pltpu.VMEM((tokens, width), BF16),
        pltpu.VMEM((tokens, features), BF16),
        pltpu.VMEM(down_factor.shape[::-1], F32),
        pltpu.VMEM(up_factor.shape, F32),
        pltpu.VMEM(weight.shape, BF16),
        pltpu.VMEM((rows, 128), BF16),
        pltpu.VMEM((rows, 128), BF16),
        pltpu.VMEM((*blocks, 32, 128), BF16),
        pltpu.VMEM((*blocks, 64, 128), BF16),
        pltpu.VMEM((RANK, features), BF16),
        pltpu.VMEM((RANK, width), BF16),
    ]
    for height in (64, 32, 16):
        scratch += [
            pltpu.VMEM((*blocks, height, 128), BF16),
            pltpu.VMEM((xy, nz, height, 128), BF16),
            pltpu.VMEM((nz, height, 128), BF16),
            pltpu.VMEM((nz - 1, height, 128), BF16),
        ]
    scratch += [
        pltpu.VMEM((96, 128), BF16),
        pltpu.VMEM((nz, 16, 128), F32),
        pltpu.VMEM((xy + 1, 16, 128), F32),
        pltpu.VMEM((*blocks, 16, 128), BF16),
        pltpu.SemaphoreType.DMA((8,)),
        pltpu.SemaphoreType.DMA((copies,)),
        pltpu.SemaphoreType.DMA((copies,)),
    ]
    fresh, outs = pl.pallas_call(
        functools.partial(kernel, sizes, rates),
        out_shape=(
            jax.ShapeDtypeStruct((96, 128), BF16),
            jax.ShapeDtypeStruct((*blocks, 16, 128), BF16),
        ),
        in_specs=[pl.BlockSpec(memory_space=pltpu.HBM)] * 7,
        out_specs=(
            pl.BlockSpec(memory_space=pltpu.VMEM),
            pl.BlockSpec(memory_space=pltpu.HBM),
        ),
        scratch_shapes=scratch,
        compiler_params=pltpu.CompilerParams(
            collective_id=0, has_side_effects=True, vmem_limit_bytes=63 * 1024 * 1024
        ),
        name="lora_step",
    )(
        learner_inputs[0], learner_cotangent[0], down_factor.T, up_factor, weight,
        context[0].reshape(rows, -1), residual[0].reshape(rows, features),
    )
    new_down, new_up, decoded = pl.pallas_call(
        finish,
        out_shape=(
            jax.ShapeDtypeStruct((64, 128), BF16),
            jax.ShapeDtypeStruct((64, 64), BF16),
            jax.ShapeDtypeStruct((rows, features), BF16),
        ),
        in_specs=[pl.BlockSpec(memory_space=pltpu.VMEM)] * 2,
        out_specs=(pl.BlockSpec(memory_space=pltpu.VMEM),) * 3,
        compiler_params=pltpu.CompilerParams(vmem_limit_bytes=63 * 1024 * 1024),
        name="finish",
    )(fresh, outs)
    return new_down.T, new_up, decoded.reshape(residual.shape)


def solution(mesh):
    groups, shards = mesh.shape["group"], mesh.shape["shard"]
    nx, nz, ny = torus(shards)
    placed = (
        P("group", "shard", None),
        P("group", "shard", None),
        P("shard", None),
        P("shard", None),
        P("shard", None),
        P("group", None, None, "shard"),
        P("group", None, None, None),
    )

    def whole(learner_inputs, learner_cotangent, *others):
        tokens, width = learner_inputs.shape[1:]
        features = learner_cotangent.shape[2]
        rates = (
            0.5 * math.sqrt(RANK) / (SCALE * math.sqrt(width * features) * math.sqrt(tokens)),
            0.5 / (SCALE * math.sqrt(RANK) * math.sqrt(tokens)),
        )
        return jax.shard_map(
            functools.partial(per_device, (nx, nz, ny, groups), rates),
            mesh=mesh,
            in_specs=placed,
            out_specs=(P("shard", None), P("shard", None), P("group", None, None, None)),
            check_vma=False,
        )(learner_inputs, learner_cotangent, *others)

    return whole
```

```python
import functools
import math

import jax
import jax.numpy as jnp
from jax import lax
from jax.experimental import pallas as pl
from jax.experimental.pallas import tpu as pltpu
from jax.sharding import PartitionSpec as P

RANK = 64
SCALE = 2.0
F32 = jnp.float32
BF16 = jnp.bfloat16
NT = (((1,), (1,)), ((), ()))


def torus(shards):
    return {64: (4, 8, 2), 8: (2, 2, 2)}[shards]


def left_half(shape):
    return lax.broadcasted_iota(jnp.int32, shape, 1) < 64


def halves(even, odd):
    keep = left_half(even.shape)
    first = jnp.where(keep, even, pltpu.roll(odd, 64, 1))
    second = jnp.where(keep, pltpu.roll(even, 64, 1), odd)
    return first, second


def kernel(
    sizes, rates,
    x_hbm, c_hbm, down_hbm, up_hbm, w_hbm, ctx_hbm, res_hbm,
    new_ref, out_hbm,
    x_v, c_v, down_v, up_v, w_v, ctx_v, res_v,
    up_all, down_all, up_flat, down_flat,
    gd, rd, sd, qd, gu, ru, su, qu,
    base, rb, sb, qb, fresh, tz, txy, outs,
    base_line, up_line, frozen, squares,
    local_sem, send_sem, recv_sem,
):
    nx, nz, ny, groups = sizes
    group = lax.axis_index("group")
    shard = lax.axis_index("shard")
    y = lax.rem(shard, ny)
    z = lax.rem(shard // ny, nz)
    x = shard // (ny * nz)
    other = 1 - y
    learner = group == 0
    helper_group = jnp.where(other == 1, groups - 2, 2)
    helper = group == jnp.where(y == 1, groups - 2, 2)

    def at(xx, zz, yy):
        return (xx * nz + zz) * ny + yy

    def x_to(d):
        return lax.rem(x + d, nx)

    def z_to(d):
        return lax.rem(z + d, nz)

    def y_to(d):
        return lax.rem(y + d, ny)

    def hops(d, n):
        return min(d, n - d)

    line = sorted(range(1, nz), key=lambda d: -hops(d, nz))
    rows = sorted(range(nx), key=lambda d: -hops(d, nx))
    plane = [(dx, dy) for dx in rows for dy in (1, 0) if (dx, dy) != (0, 0)]

    local = [
        pltpu.make_async_copy(src, dst, local_sem.at[i])
        for i, (src, dst) in enumerate(
            [
                (up_hbm, up_v),
                (down_hbm, down_v),
                (ctx_hbm, ctx_v),
                (w_hbm, w_v),
                (res_hbm.at[:, pl.ds(pl.multiple_of(x * (nz * 128), 128), nz * 128)], res_v),
                (c_hbm, c_v),
                (x_hbm, x_v),
            ]
        )
    ]
    barrier = pltpu.get_barrier_semaphore()
    peers = [at(x, z_to(d), y) for d in line] + [at(x_to(dx), z, y_to(dy)) for dx, dy in plane]
    for peer in peers:
        pl.semaphore_signal(
            barrier, inc=1, device_id={"shard": peer}, device_id_type=pl.DeviceIdType.MESH
        )

    @pl.when(jnp.logical_not(learner))
    def _():
        pl.semaphore_signal(
            barrier, inc=1, device_id={"group": 0}, device_id_type=pl.DeviceIdType.MESH
        )

    @pl.when(learner)
    def _():
        for d in range(nx):
            pl.semaphore_signal(
                barrier, inc=1, device_id={"group": helper_group, "shard": at(x_to(d), z, other)},
                device_id_type=pl.DeviceIdType.MESH,
            )

    for copy in local[:5]:
        copy.start()

    @pl.when(learner)
    def _():
        local[5].start()
        local[6].start()

    used = [0]

    def remote(src, dst, peer):
        k = used[0]
        used[0] += 1
        return pltpu.make_async_remote_copy(
            src_ref=src, dst_ref=dst, send_sem=send_sem.at[k], recv_sem=recv_sem.at[k],
            device_id={"shard": peer}, device_id_type=pl.DeviceIdType.MESH,
        )

    def along(ref_of, dst_of):
        return [remote(ref_of(z_to(d)), dst_of(i, d), at(x, z_to(d), y)) for i, d in enumerate(line)]

    def across(ref_of, dst_of):
        return [
            remote(ref_of(x_to(dx), y_to(dy)), dst_of(i), at(x_to(dx), z, y_to(dy)))
            for i, (dx, dy) in enumerate(plane)
        ]

    def beside(ref):
        return [remote(ref, ref, at(x_to(d), z, y)) for d in rows if d]

    def helped(ref):
        copies = []
        for d in rows:
            k = used[0]
            used[0] += 1
            copies.append(
                pltpu.make_async_remote_copy(
                    src_ref=ref, dst_ref=ref, send_sem=send_sem.at[k], recv_sem=recv_sem.at[k],
                    device_id={"group": 0, "shard": at(x_to(d), z, other)},
                    device_id_type=pl.DeviceIdType.MESH,
                )
            )
        return copies

    def start(copies, started):
        for copy in copies:
            copy.start()
        started.extend(copies)

    def arrive(copies):
        for copy in copies:
            copy.wait_recv()

    def sent(started):
        for copy in started:
            copy.wait_send()

    learnt, lent, decoded = [], [], []

    up_z = along(lambda zz: up_all.at[y, x, z], lambda i, d: up_all.at[y, x, z])
    down_z = along(lambda zz: down_all.at[y, x, z], lambda i, d: down_all.at[y, x, z])
    up_x = beside(up_all.at[y, x])
    up_y = helped(up_all.at[y, x])
    down_x = beside(down_all.at[y, x])
    down_y = helped(down_all.at[y, x])
    gd_xy = across(lambda xx, yy: gd.at[yy, xx], lambda i: rd.at[i])
    gd_z = along(lambda zz: sd.at[zz], lambda i, d: qd.at[i])
    gu_xy = across(lambda xx, yy: gu.at[yy, xx], lambda i: ru.at[i])
    gu_z = along(lambda zz: su.at[zz], lambda i, d: qu.at[i])
    base_xy = across(lambda xx, yy: base.at[yy, xx], lambda i: rb.at[i])
    base_z = along(lambda zz: sb.at[zz], lambda i, d: qb.at[i])
    base_g = along(lambda zz: base_line.at[z], lambda i, d: base_line.at[z])
    up_g = along(lambda zz: up_line.at[z], lambda i, d: up_line.at[z])
    low_z = along(lambda zz: tz.at[0], lambda i, d: tz.at[i + 1])
    low_xy = across(lambda xx, yy: txy.at[0], lambda i: txy.at[i + 1])
    out_xy = across(lambda xx, yy: outs, lambda i: out_hbm.at[y, x])
    out_own = pltpu.make_async_copy(outs, out_hbm.at[y, x], local_sem.at[7])

    def spread(part, k):
        order = [g for hi in (2, 1, 3, 0) for g in (2 * hi, 2 * hi + 1) if 0 < g < groups]
        return [
            pltpu.make_async_remote_copy(
                src_ref=part, dst_ref=part, send_sem=send_sem.at[k + i], recv_sem=recv_sem.at[k],
                device_id={"group": g}, device_id_type=pl.DeviceIdType.MESH,
            )
            for i, g in enumerate(order)
        ]

    down_spread = spread(fresh, used[0])
    up_spread = spread(up_line.at[z], used[0] + groups - 1)

    def summed(own, others, index=()):
        total = own.astype(F32)
        for i in range(others.shape[0]):
            total = total + others[(i, *index)].astype(F32)
        return total

    def packed_up():
        up_t = up_v[...].T
        up_t = jnp.concatenate([up_t, jnp.zeros_like(up_t)], axis=1)
        return halves(up_t[0:32], up_t[32:64])[0]

    def project(xx, _):
        for zz in range(nz):
            column = pl.multiple_of((xx * nz + zz) * 128, 128)
            block = jnp.dot(ctx_v[...], w_v[:, pl.ds(column, 128)], preferred_element_type=F32)
            even, odd = halves(block[0:16], block[16:32])
            base[0, xx, zz] = even.astype(BF16)
            base[1, xx, zz] = odd.astype(BF16)
        return 0

    def base_lines():
        arrive(base_xy)
        for d, copy in zip(line, base_z):
            zz = z_to(d)
            sb[zz] = summed(base[y, x, zz], rb, (zz,)).astype(BF16)
            copy.start()
        sb[z] = summed(base[y, x, z], rb, (z,)).astype(BF16)

    def base_total():
        arrive(base_z)
        base_line[z] = summed(sb[z], qb).astype(BF16)
        start(base_g, [])

    def freeze():
        arrive(base_g)
        local[4].wait()
        for zz in range(nz):
            held = res_v[:, zz * 128 : (zz + 1) * 128].astype(F32)
            even, odd = halves(held[0:16], held[16:32])
            frozen[:, zz * 128 : (zz + 1) * 128] = base_line[zz].astype(F32) + jnp.where(
                y == 0, even, odd
            )

    local[0].wait()
    packed = packed_up()
    pl.semaphore_wait(
        barrier,
        len(peers) + jnp.where(learner, groups - 1, 0) + jnp.where(helper, nx, 0),
    )

    local[1].wait()

    @pl.when(jnp.logical_or(learner, helper))
    def _():
        up_all[y, x, z] = packed.astype(BF16)
        for copy in up_z:
            copy.start()
        down_all[y, x, z] = down_v[...].astype(BF16)
        for copy in down_z:
            copy.start()
        arrive(up_z)

        @pl.when(learner)
        def _():
            start(up_x, learnt)

        @pl.when(helper)
        def _():
            start(up_y, lent)

        arrive(down_z)

        @pl.when(learner)
        def _():
            start(down_x, learnt)

        @pl.when(helper)
        def _():
            start(down_y, lent)

    learnt.extend(up_z + down_z)
    lent.extend(up_z + down_z)
    local[2].wait()
    local[3].wait()
    lax.fori_loop(0, nx, project, 0)

    @pl.when(jnp.logical_not(learner))
    def _():
        start(base_xy, [])
        base_lines()
        base_total()
        freeze()

    @pl.when(learner)
    def _():
        local[5].wait()
        arrive(up_x)
        arrive(up_y)

        def unpack_up(xx, _):
            for zz in range(nz):
                column = pl.multiple_of((xx * nz + zz) * 128, 128)
                top, low = halves(
                    up_all[0, xx, zz].astype(F32), up_all[1, xx, zz].astype(F32)
                )
                up_flat[:, pl.ds(column, 128)] = jnp.concatenate([top, low], axis=0).astype(BF16)
            return 0

        lax.fori_loop(0, nx, unpack_up, 0)
        lifted = lax.dot_general(
            up_flat[...], c_v[...], NT, preferred_element_type=F32
        ).astype(BF16)
        local[6].wait()
        for dx in rows:
            xx = x_to(dx)
            for zz in range(nz):
                column = pl.multiple_of((xx * nz + zz) * 256, 256)
                block = jnp.dot(lifted, x_v[:, pl.ds(column, 256)], preferred_element_type=F32)
                block = block.astype(BF16)
                gd[0, xx, zz] = block[:, 0:128]
                gd[1, xx, zz] = block[:, 128:256]
            start([c for c, p in zip(gd_xy, plane) if p[0] == dx], learnt)
        start(base_xy, [])
        arrive(down_x)
        arrive(down_y)

        def flatten(xx, _):
            for zz in range(nz):
                column = pl.multiple_of((xx * nz + zz) * 256, 256)
                down_flat[:, pl.ds(column, 256)] = jnp.concatenate(
                    [down_all[0, xx, zz], down_all[1, xx, zz]], axis=1
                )
            return 0

        lax.fori_loop(0, nx, flatten, 0)
        lowered = lax.dot_general(
            down_flat[...], x_v[...], NT, preferred_element_type=F32
        ).astype(BF16)
        for dx in rows:
            xx = x_to(dx)
            for zz in range(nz):
                column = pl.multiple_of((xx * nz + zz) * 128, 128)
                block = jnp.dot(lowered, c_v[:, pl.ds(column, 128)], preferred_element_type=F32)
                even, odd = halves(block[0:32], block[32:64])
                gu[0, xx, zz] = even.astype(BF16)
                gu[1, xx, zz] = odd.astype(BF16)
            start([c for c, p in zip(gu_xy, plane) if p[0] == dx], learnt)
        arrive(gd_xy)
        for d, copy in zip(line, gd_z):
            zz = z_to(d)
            sd[zz] = summed(gd[y, x, zz], rd, (zz,)).astype(BF16)
            start([copy], learnt)
        sd[z] = summed(gd[y, x, z], rd, (z,)).astype(BF16)
        base_lines()
        arrive(gd_z)
        total = summed(sd[z], qd)
        fresh[...] = (down_v[...] - rates[0] * (SCALE * total)).astype(BF16)
        start(down_spread, learnt)
        arrive(gu_xy)
        for d, copy in zip(line, gu_z):
            zz = z_to(d)
            su[zz] = summed(gu[y, x, zz], ru, (zz,)).astype(BF16)
            start([copy], learnt)
        su[z] = summed(gu[y, x, z], ru, (z,)).astype(BF16)

    decoded.extend(base_xy + base_z + base_g)

    @pl.when(jnp.logical_not(learner))
    def _():
        down_spread[0].wait_recv()

    new_down = fresh[...]
    nothing = jnp.zeros_like(new_down)
    first = jnp.concatenate([new_down, nothing], axis=0)
    second = jnp.concatenate([nothing, new_down], axis=0)
    tz[0] = lax.dot_general(
        ctx_v[0:16], first, NT, preferred_element_type=F32
    ) + lax.dot_general(ctx_v[16:32], second, NT, preferred_element_type=F32)
    start(low_z, decoded)

    @pl.when(learner)
    def _():
        base_total()
        arrive(gu_z)
        up_line[z] = (packed - rates[1] * (SCALE * summed(su[z], qu))).astype(BF16)
        start(up_spread, learnt)
        start(up_g, [])

    arrive(low_z)
    txy[0] = jnp.sum(tz[...], axis=0)
    start(low_xy, decoded)

    @pl.when(learner)
    def _():
        freeze()

    @pl.when(jnp.logical_not(learner))
    def _():
        up_spread[0].wait_recv()
        start(up_g, [])

    decoded.extend(up_g)
    new_ref[0:64] = fresh[...]
    new_ref[64:96] = up_line[z]
    arrive(up_g)
    for zz in range(nz):
        new_up = up_line[zz].astype(F32)
        turned = pltpu.roll(new_up, 64, 1)
        keep = left_half(new_up.shape)
        squares[:, zz * 128 : (zz + 1) * 128] = jnp.concatenate(
            [
                jnp.where(keep, new_up, 0.0),
                jnp.where(keep, turned, 0.0),
                jnp.where(keep, 0.0, turned),
                jnp.where(keep, 0.0, new_up),
            ],
            axis=0,
        ).astype(BF16)
    arrive(low_xy)
    lowered_rows = jnp.sum(txy[...], axis=0).astype(BF16)
    delta = jnp.dot(lowered_rows, squares[...], preferred_element_type=F32)
    for zz in range(nz):
        part = slice(zz * 128, (zz + 1) * 128)
        outs[zz] = (frozen[:, part] + SCALE * delta[:, part]).astype(BF16)
    start(out_xy, decoded)
    out_own.start()
    arrive(out_xy)

    out_own.wait()
    sent(decoded)

    @pl.when(learner)
    def _():
        sent(learnt)

    @pl.when(helper)
    def _():
        sent(lent)


def finish(fresh_ref, outs_ref, down_ref, up_ref, dec_ref):
    ny, nx, nz = outs_ref.shape[:3]
    down_ref[...] = fresh_ref[0:64]
    packed = fresh_ref[64:96].astype(F32)
    up_t = jnp.concatenate([packed, pltpu.roll(packed, 64, 1)], axis=0)
    up_ref[...] = up_t.T[0:64].astype(BF16)
    for xx in range(nx):
        for zz in range(nz):
            column = (xx * nz + zz) * 128
            top, low = halves(outs_ref[0, xx, zz].astype(F32), outs_ref[1, xx, zz].astype(F32))
            dec_ref[0:16, column : column + 128] = top.astype(BF16)
            dec_ref[16:32, column : column + 128] = low.astype(BF16)


def per_device(
    sizes, rates,
    learner_inputs, learner_cotangent, down_factor, up_factor, weight, context, residual
):
    nx, nz, ny, groups = sizes
    tokens, width = learner_inputs.shape[1:]
    features = learner_cotangent.shape[2]
    rows = context.shape[1] * context.shape[2]
    xy = nx * ny - 1
    copies = 8 * (nz - 1) + 5 * xy + 2 * (2 * nx - 1) + 2 * (groups - 1)
    blocks = (ny, nx, nz)
    scratch = [
        pltpu.VMEM((tokens, width), BF16),
        pltpu.VMEM((tokens, features), BF16),
        pltpu.VMEM(down_factor.shape[::-1], F32),
        pltpu.VMEM(up_factor.shape, F32),
        pltpu.VMEM(weight.shape, BF16),
        pltpu.VMEM((rows, 128), BF16),
        pltpu.VMEM((rows, nz * 128), BF16),
        pltpu.VMEM((*blocks, 32, 128), BF16),
        pltpu.VMEM((*blocks, 64, 128), BF16),
        pltpu.VMEM((RANK, features), BF16),
        pltpu.VMEM((RANK, width), BF16),
    ]
    for height in (64, 32, 16):
        scratch += [
            pltpu.VMEM((*blocks, height, 128), BF16),
            pltpu.VMEM((xy, nz, height, 128), BF16),
            pltpu.VMEM((nz, height, 128), BF16),
            pltpu.VMEM((nz - 1, height, 128), BF16),
        ]
    scratch += [
        pltpu.VMEM((64, 128), BF16),
        pltpu.VMEM((nz, 16, 128), F32),
        pltpu.VMEM((xy + 1, 16, 128), F32),
        pltpu.VMEM((nz, 16, 128), BF16),
        pltpu.VMEM((nz, 16, 128), BF16),
        pltpu.VMEM((nz, 32, 128), BF16),
        pltpu.VMEM((16, nz * 128), F32),
        pltpu.VMEM((128, nz * 128), BF16),
        pltpu.SemaphoreType.DMA((8,)),
        pltpu.SemaphoreType.DMA((copies,)),
        pltpu.SemaphoreType.DMA((copies,)),
    ]
    fresh, outs = pl.pallas_call(
        functools.partial(kernel, sizes, rates),
        out_shape=(
            jax.ShapeDtypeStruct((96, 128), BF16),
            jax.ShapeDtypeStruct((*blocks, 16, 128), BF16),
        ),
        in_specs=[pl.BlockSpec(memory_space=pltpu.HBM)] * 7,
        out_specs=(
            pl.BlockSpec(memory_space=pltpu.VMEM),
            pl.BlockSpec(memory_space=pltpu.HBM),
        ),
        scratch_shapes=scratch,
        compiler_params=pltpu.CompilerParams(
            collective_id=0, has_side_effects=True, vmem_limit_bytes=63 * 1024 * 1024
        ),
        name="lora_step",
    )(
        learner_inputs[0], learner_cotangent[0], down_factor.T, up_factor, weight,
        context[0].reshape(rows, -1), residual[0].reshape(rows, features),
    )
    new_down, new_up, decoded = pl.pallas_call(
        finish,
        out_shape=(
            jax.ShapeDtypeStruct((64, 128), BF16),
            jax.ShapeDtypeStruct((64, 64), BF16),
            jax.ShapeDtypeStruct((rows, features), BF16),
        ),
        in_specs=[pl.BlockSpec(memory_space=pltpu.VMEM)] * 2,
        out_specs=(pl.BlockSpec(memory_space=pltpu.VMEM),) * 3,
        compiler_params=pltpu.CompilerParams(vmem_limit_bytes=63 * 1024 * 1024),
        name="finish",
    )(fresh, outs)
    return new_down.T, new_up, decoded.reshape(residual.shape)


def solution(mesh):
    groups, shards = mesh.shape["group"], mesh.shape["shard"]
    nx, nz, ny = torus(shards)
    placed = (
        P("group", "shard", None),
        P("group", "shard", None),
        P("shard", None),
        P("shard", None),
        P("shard", None),
        P("group", None, None, "shard"),
        P("group", None, None, None),
    )

    def whole(learner_inputs, learner_cotangent, *others):
        tokens, width = learner_inputs.shape[1:]
        features = learner_cotangent.shape[2]
        rates = (
            0.5 * math.sqrt(RANK) / (SCALE * math.sqrt(width * features) * math.sqrt(tokens)),
            0.5 / (SCALE * math.sqrt(RANK) * math.sqrt(tokens)),
        )
        return jax.shard_map(
            functools.partial(per_device, (nx, nz, ny, groups), rates),
            mesh=mesh,
            in_specs=placed,
            out_specs=(P("shard", None), P("shard", None), P("group", None, None, None)),
            check_vma=False,
        )(learner_inputs, learner_cotangent, *others)

    return whole
```

```python
import functools
import math

import jax
import jax.numpy as jnp
from jax import lax
from jax.experimental import pallas as pl
from jax.experimental.pallas import tpu as pltpu
from jax.sharding import PartitionSpec as P

RANK = 64
SCALE = 2.0
F32 = jnp.float32
BF16 = jnp.bfloat16
NT = (((1,), (1,)), ((), ()))


def torus(shards):
    return {64: (4, 8, 2), 8: (2, 2, 2)}[shards]


def left_half(shape):
    return lax.broadcasted_iota(jnp.int32, shape, 1) < 64


def halves(even, odd):
    keep = left_half(even.shape)
    first = jnp.where(keep, even, pltpu.roll(odd, 64, 1))
    second = jnp.where(keep, pltpu.roll(even, 64, 1), odd)
    return first, second


def kernel(
    sizes, rates,
    x_hbm, c_hbm, down_hbm, up_hbm, w_hbm, ctx_hbm, res_hbm,
    new_hbm, out_hbm,
    x_v, c_v, down_v, up_v, w_v, ctx_v, res_v,
    up_all, down_all, up_flat, down_flat,
    gd, rd, sd, qd, gu, ru, su, qu,
    base, rb, sb, qb, fresh, tz, txy, outs,
    base_line, up_line, frozen, squares,
    local_sem, send_sem, recv_sem, ready_sem,
):
    nx, nz, ny, groups = sizes
    group = lax.axis_index("group")
    shard = lax.axis_index("shard")
    y = lax.rem(shard, ny)
    z = lax.rem(shard // ny, nz)
    x = shard // (ny * nz)
    other = 1 - y
    learner = group == 0
    helper_group = jnp.where(other == 1, groups - 2, 2)
    helper = group == jnp.where(y == 1, groups - 2, 2)

    def at(xx, zz, yy):
        return (xx * nz + zz) * ny + yy

    def x_to(d):
        return lax.rem(x + d, nx)

    def z_to(d):
        return lax.rem(z + d, nz)

    def y_to(d):
        return lax.rem(y + d, ny)

    def hops(d, n):
        return min(d, n - d)

    line = sorted(range(1, nz), key=lambda d: -hops(d, nz))
    rows = sorted(range(nx), key=lambda d: -hops(d, nx))
    plane = [(dx, dy) for dx in rows for dy in (1, 0) if (dx, dy) != (0, 0)]

    local = [
        pltpu.make_async_copy(src, dst, local_sem.at[i])
        for i, (src, dst) in enumerate(
            [
                (up_hbm, up_v),
                (down_hbm, down_v),
                (ctx_hbm, ctx_v),
                (w_hbm, w_v),
                (res_hbm.at[:, pl.ds(pl.multiple_of(x * (nz * 128), 128), nz * 128)], res_v),
                (c_hbm, c_v),
                (x_hbm, x_v),
            ]
        )
    ]
    barrier = pltpu.get_barrier_semaphore()
    peers = [at(x, z_to(d), y) for d in line] + [at(x_to(dx), z, y_to(dy)) for dx, dy in plane]
    for peer in peers:
        pl.semaphore_signal(
            barrier, inc=1, device_id={"shard": peer}, device_id_type=pl.DeviceIdType.MESH
        )

    @pl.when(learner)
    def _():
        for d in range(nx):
            pl.semaphore_signal(
                barrier, inc=1, device_id={"group": helper_group, "shard": at(x_to(d), z, other)},
                device_id_type=pl.DeviceIdType.MESH,
            )
        for g in range(1, groups):
            pl.semaphore_signal(
                barrier, inc=1, device_id={"group": g}, device_id_type=pl.DeviceIdType.MESH
            )

    for copy in local[:5]:
        copy.start()

    @pl.when(learner)
    def _():
        local[5].start()
        local[6].start()

    used = [0]

    def remote(src, dst, peer):
        k = used[0]
        used[0] += 1
        return pltpu.make_async_remote_copy(
            src_ref=src, dst_ref=dst, send_sem=send_sem.at[k], recv_sem=recv_sem.at[k],
            device_id={"shard": peer}, device_id_type=pl.DeviceIdType.MESH,
        )

    def along(ref_of, dst_of):
        return [remote(ref_of(z_to(d)), dst_of(i, d), at(x, z_to(d), y)) for i, d in enumerate(line)]

    def across(ref_of, dst_of):
        return [
            remote(ref_of(x_to(dx), y_to(dy)), dst_of(i), at(x_to(dx), z, y_to(dy)))
            for i, (dx, dy) in enumerate(plane)
        ]

    def beside(ref):
        return [remote(ref, ref, at(x_to(d), z, y)) for d in rows if d]

    def helped(ref):
        copies = []
        for d in rows:
            k = used[0]
            used[0] += 1
            copies.append(
                pltpu.make_async_remote_copy(
                    src_ref=ref, dst_ref=ref, send_sem=send_sem.at[k], recv_sem=recv_sem.at[k],
                    device_id={"group": 0, "shard": at(x_to(d), z, other)},
                    device_id_type=pl.DeviceIdType.MESH,
                )
            )
        return copies

    def start(copies, started):
        for copy in copies:
            copy.start()
        started.extend(copies)

    def arrive(copies):
        for copy in copies:
            copy.wait_recv()

    def sent(started):
        for copy in started:
            copy.wait_send()

    learnt, lent, decoded = [], [], []

    up_z = along(lambda zz: up_all.at[y, x, z], lambda i, d: up_all.at[y, x, z])
    down_z = along(lambda zz: down_all.at[y, x, z], lambda i, d: down_all.at[y, x, z])
    up_x = beside(up_all.at[y, x])
    up_y = helped(up_all.at[y, x])
    down_x = beside(down_all.at[y, x])
    down_y = helped(down_all.at[y, x])
    gd_xy = across(lambda xx, yy: gd.at[yy, xx], lambda i: rd.at[i])
    gd_z = along(lambda zz: sd.at[zz], lambda i, d: qd.at[i])
    gu_xy = across(lambda xx, yy: gu.at[yy, xx], lambda i: ru.at[i])
    gu_z = along(lambda zz: su.at[zz], lambda i, d: qu.at[i])
    base_xy = across(lambda xx, yy: base.at[yy, xx], lambda i: rb.at[i])
    base_z = along(lambda zz: sb.at[zz], lambda i, d: qb.at[i])
    base_g = along(lambda zz: base_line.at[z], lambda i, d: base_line.at[z])
    up_g = along(lambda zz: up_line.at[z], lambda i, d: up_line.at[z])
    low_z = along(lambda zz: tz.at[0], lambda i, d: tz.at[i + 1])
    low_xy = across(lambda xx, yy: txy.at[0], lambda i: txy.at[i + 1])
    out_xy = across(lambda xx, yy: outs, lambda i: out_hbm.at[y, x])
    out_own = pltpu.make_async_copy(outs, out_hbm.at[y, x], local_sem.at[7])

    def spread(part, k):
        order = [g for hi in (2, 1, 3, 0) for g in (2 * hi, 2 * hi + 1) if 0 < g < groups]
        return [
            pltpu.make_async_remote_copy(
                src_ref=part, dst_ref=part, send_sem=send_sem.at[k + i], recv_sem=recv_sem.at[k],
                device_id={"group": g}, device_id_type=pl.DeviceIdType.MESH,
            )
            for i, g in enumerate(order)
        ]

    down_spread = spread(fresh, used[0])
    up_spread = spread(up_line.at[z], used[0] + groups - 1)

    def summed(own, others, index=()):
        total = own.astype(F32)
        for i in range(others.shape[0]):
            total = total + others[(i, *index)].astype(F32)
        return total

    def packed_up():
        up_t = up_v[...].T
        up_t = jnp.concatenate([up_t, jnp.zeros_like(up_t)], axis=1)
        return halves(up_t[0:32], up_t[32:64])[0]

    def project(xx, _):
        for zz in range(nz):
            column = pl.multiple_of((xx * nz + zz) * 128, 128)
            block = jnp.dot(ctx_v[...], w_v[:, pl.ds(column, 128)], preferred_element_type=F32)
            even, odd = halves(block[0:16], block[16:32])
            base[0, xx, zz] = even.astype(BF16)
            base[1, xx, zz] = odd.astype(BF16)
        return 0

    def base_lines():
        arrive(base_xy)
        for d, copy in zip(line, base_z):
            zz = z_to(d)
            sb[zz] = summed(base[y, x, zz], rb, (zz,)).astype(BF16)
            copy.start()
        sb[z] = summed(base[y, x, z], rb, (z,)).astype(BF16)

    def base_total():
        arrive(base_z)
        base_line[z] = summed(sb[z], qb).astype(BF16)
        start(base_g, [])

    def freeze():
        arrive(base_g)
        local[4].wait()
        for zz in range(nz):
            held = res_v[:, zz * 128 : (zz + 1) * 128].astype(F32)
            even, odd = halves(held[0:16], held[16:32])
            frozen[:, zz * 128 : (zz + 1) * 128] = base_line[zz].astype(F32) + jnp.where(
                y == 0, even, odd
            )

    local[0].wait()
    packed = packed_up()
    pl.semaphore_wait(
        barrier,
        len(peers) + jnp.where(learner, 0, 1) + jnp.where(helper, nx, 0),
    )

    @pl.when(jnp.logical_not(learner))
    def _():
        pl.semaphore_signal(
            ready_sem, inc=1, device_id={"group": 0}, device_id_type=pl.DeviceIdType.MESH
        )

    local[1].wait()

    @pl.when(jnp.logical_or(learner, helper))
    def _():
        up_all[y, x, z] = packed.astype(BF16)
        for copy in up_z:
            copy.start()
        down_all[y, x, z] = down_v[...].astype(BF16)
        for copy in down_z:
            copy.start()
        arrive(up_z)

        @pl.when(learner)
        def _():
            start(up_x, learnt)

        @pl.when(helper)
        def _():
            start(up_y, lent)

        arrive(down_z)

        @pl.when(learner)
        def _():
            start(down_x, learnt)

        @pl.when(helper)
        def _():
            start(down_y, lent)

    learnt.extend(up_z + down_z)
    lent.extend(up_z + down_z)
    local[2].wait()
    local[3].wait()
    lax.fori_loop(0, nx, project, 0)

    @pl.when(jnp.logical_not(learner))
    def _():
        start(base_xy, [])
        base_lines()
        base_total()
        freeze()

    @pl.when(learner)
    def _():
        local[5].wait()
        arrive(up_x)
        arrive(up_y)

        def unpack_up(xx, _):
            for zz in range(nz):
                column = pl.multiple_of((xx * nz + zz) * 128, 128)
                top, low = halves(
                    up_all[0, xx, zz].astype(F32), up_all[1, xx, zz].astype(F32)
                )
                up_flat[:, pl.ds(column, 128)] = jnp.concatenate([top, low], axis=0).astype(BF16)
            return 0

        lax.fori_loop(0, nx, unpack_up, 0)
        lifted = lax.dot_general(
            up_flat[...], c_v[...], NT, preferred_element_type=F32
        ).astype(BF16)
        local[6].wait()
        for dx in rows:
            xx = x_to(dx)
            for zz in range(nz):
                column = pl.multiple_of((xx * nz + zz) * 256, 256)
                block = jnp.dot(lifted, x_v[:, pl.ds(column, 256)], preferred_element_type=F32)
                block = block.astype(BF16)
                gd[0, xx, zz] = block[:, 0:128]
                gd[1, xx, zz] = block[:, 128:256]
            start([c for c, p in zip(gd_xy, plane) if p[0] == dx], learnt)
        start(base_xy, [])
        arrive(down_x)
        arrive(down_y)

        def flatten(xx, _):
            for zz in range(nz):
                column = pl.multiple_of((xx * nz + zz) * 256, 256)
                down_flat[:, pl.ds(column, 256)] = jnp.concatenate(
                    [down_all[0, xx, zz], down_all[1, xx, zz]], axis=1
                )
            return 0

        lax.fori_loop(0, nx, flatten, 0)
        lowered = lax.dot_general(
            down_flat[...], x_v[...], NT, preferred_element_type=F32
        ).astype(BF16)
        for dx in rows:
            xx = x_to(dx)
            for zz in range(nz):
                column = pl.multiple_of((xx * nz + zz) * 128, 128)
                block = jnp.dot(lowered, c_v[:, pl.ds(column, 128)], preferred_element_type=F32)
                even, odd = halves(block[0:32], block[32:64])
                gu[0, xx, zz] = even.astype(BF16)
                gu[1, xx, zz] = odd.astype(BF16)
            start([c for c, p in zip(gu_xy, plane) if p[0] == dx], learnt)
        arrive(gd_xy)
        for d, copy in zip(line, gd_z):
            zz = z_to(d)
            sd[zz] = summed(gd[y, x, zz], rd, (zz,)).astype(BF16)
            start([copy], learnt)
        sd[z] = summed(gd[y, x, z], rd, (z,)).astype(BF16)
        base_lines()
        arrive(gd_z)
        total = summed(sd[z], qd)
        fresh[...] = (down_v[...] - rates[0] * (SCALE * total)).astype(BF16)
        pl.semaphore_wait(ready_sem, groups - 1)
        start(down_spread, learnt)
        arrive(gu_xy)
        for d, copy in zip(line, gu_z):
            zz = z_to(d)
            su[zz] = summed(gu[y, x, zz], ru, (zz,)).astype(BF16)
            start([copy], learnt)
        su[z] = summed(gu[y, x, z], ru, (z,)).astype(BF16)

    decoded.extend(base_xy + base_z + base_g)

    @pl.when(jnp.logical_not(learner))
    def _():
        down_spread[0].wait_recv()

    new_down = fresh[...]
    nothing = jnp.zeros_like(new_down)
    first = jnp.concatenate([new_down, nothing], axis=0)
    second = jnp.concatenate([nothing, new_down], axis=0)
    tz[0] = lax.dot_general(
        ctx_v[0:16], first, NT, preferred_element_type=F32
    ) + lax.dot_general(ctx_v[16:32], second, NT, preferred_element_type=F32)
    start(low_z, decoded)

    @pl.when(learner)
    def _():
        base_total()
        arrive(gu_z)
        up_line[z] = (packed - rates[1] * (SCALE * summed(su[z], qu))).astype(BF16)
        start(up_spread, learnt)
        start(up_g, [])

    arrive(low_z)
    txy[0] = jnp.sum(tz[...], axis=0)
    start(low_xy, decoded)

    @pl.when(learner)
    def _():
        freeze()

    @pl.when(jnp.logical_not(learner))
    def _():
        up_spread[0].wait_recv()
        start(up_g, [])

    written = [
        pltpu.make_async_copy(fresh, new_hbm.at[0:64], local_sem.at[8]),
        pltpu.make_async_copy(up_line.at[z], new_hbm.at[64:96], local_sem.at[9]),
    ]
    for copy in written:
        copy.start()
    sent([copy for copy in decoded if not any(copy is late for late in low_xy)])

    @pl.when(learner)
    def _():
        sent(learnt)

    @pl.when(helper)
    def _():
        sent(lent)

    arrive(up_g)
    for zz in range(nz):
        new_up = up_line[zz].astype(F32)
        turned = pltpu.roll(new_up, 64, 1)
        keep = left_half(new_up.shape)
        squares[:, zz * 128 : (zz + 1) * 128] = jnp.concatenate(
            [
                jnp.where(keep, new_up, 0.0),
                jnp.where(keep, turned, 0.0),
                jnp.where(keep, 0.0, turned),
                jnp.where(keep, 0.0, new_up),
            ],
            axis=0,
        ).astype(BF16)
    arrive(low_xy)
    lowered_rows = jnp.sum(txy[...], axis=0).astype(BF16)
    delta = jnp.dot(lowered_rows, squares[...], preferred_element_type=F32)
    for zz in range(nz):
        part = slice(zz * 128, (zz + 1) * 128)
        outs[zz] = (frozen[:, part] + SCALE * delta[:, part]).astype(BF16)
    start(out_xy, decoded)
    out_own.start()
    arrive(out_xy)

    out_own.wait()
    for copy in written:
        copy.wait()
    sent(up_g + low_xy + out_xy)


def finish(fresh_ref, outs_ref, down_ref, up_ref, dec_ref):
    ny, nx, nz = outs_ref.shape[:3]
    down_ref[...] = fresh_ref[0:64]
    packed = fresh_ref[64:96].astype(F32)
    up_t = jnp.concatenate([packed, pltpu.roll(packed, 64, 1)], axis=0)
    up_ref[...] = up_t.T[0:64].astype(BF16)
    for xx in range(nx):
        for zz in range(nz):
            column = (xx * nz + zz) * 128
            top, low = halves(outs_ref[0, xx, zz].astype(F32), outs_ref[1, xx, zz].astype(F32))
            dec_ref[0:16, column : column + 128] = top.astype(BF16)
            dec_ref[16:32, column : column + 128] = low.astype(BF16)


def per_device(
    sizes, rates,
    learner_inputs, learner_cotangent, down_factor, up_factor, weight, context, residual
):
    nx, nz, ny, groups = sizes
    tokens, width = learner_inputs.shape[1:]
    features = learner_cotangent.shape[2]
    rows = context.shape[1] * context.shape[2]
    xy = nx * ny - 1
    copies = 8 * (nz - 1) + 5 * xy + 2 * (2 * nx - 1) + 2 * (groups - 1)
    blocks = (ny, nx, nz)
    scratch = [
        pltpu.VMEM((tokens, width), BF16),
        pltpu.VMEM((tokens, features), BF16),
        pltpu.VMEM(down_factor.shape[::-1], F32),
        pltpu.VMEM(up_factor.shape, F32),
        pltpu.VMEM(weight.shape, BF16),
        pltpu.VMEM((rows, 128), BF16),
        pltpu.VMEM((rows, nz * 128), BF16),
        pltpu.VMEM((*blocks, 32, 128), BF16),
        pltpu.VMEM((*blocks, 64, 128), BF16),
        pltpu.VMEM((RANK, features), BF16),
        pltpu.VMEM((RANK, width), BF16),
    ]
    for height in (64, 32, 16):
        scratch += [
            pltpu.VMEM((*blocks, height, 128), BF16),
            pltpu.VMEM((xy, nz, height, 128), BF16),
            pltpu.VMEM((nz, height, 128), BF16),
            pltpu.VMEM((nz - 1, height, 128), BF16),
        ]
    scratch += [
        pltpu.VMEM((64, 128), BF16),
        pltpu.VMEM((nz, 16, 128), F32),
        pltpu.VMEM((xy + 1, 16, 128), F32),
        pltpu.VMEM((nz, 16, 128), BF16),
        pltpu.VMEM((nz, 16, 128), BF16),
        pltpu.VMEM((nz, 32, 128), BF16),
        pltpu.VMEM((16, nz * 128), F32),
        pltpu.VMEM((128, nz * 128), BF16),
        pltpu.SemaphoreType.DMA((10,)),
        pltpu.SemaphoreType.DMA((copies,)),
        pltpu.SemaphoreType.DMA((copies,)),
        pltpu.SemaphoreType.REGULAR,
    ]
    fresh, outs = pl.pallas_call(
        functools.partial(kernel, sizes, rates),
        out_shape=(
            jax.ShapeDtypeStruct((96, 128), BF16),
            jax.ShapeDtypeStruct((*blocks, 16, 128), BF16),
        ),
        in_specs=[pl.BlockSpec(memory_space=pltpu.HBM)] * 7,
        out_specs=(pl.BlockSpec(memory_space=pltpu.HBM),) * 2,
        scratch_shapes=scratch,
        compiler_params=pltpu.CompilerParams(
            collective_id=0, has_side_effects=True, vmem_limit_bytes=63 * 1024 * 1024
        ),
        name="lora_step",
    )(
        learner_inputs[0], learner_cotangent[0], down_factor.T, up_factor, weight,
        context[0].reshape(rows, -1), residual[0].reshape(rows, features),
    )
    new_down, new_up, decoded = pl.pallas_call(
        finish,
        out_shape=(
            jax.ShapeDtypeStruct((64, 128), BF16),
            jax.ShapeDtypeStruct((64, 64), BF16),
            jax.ShapeDtypeStruct((rows, features), BF16),
        ),
        in_specs=[pl.BlockSpec(memory_space=pltpu.VMEM)] * 2,
        out_specs=(pl.BlockSpec(memory_space=pltpu.VMEM),) * 3,
        compiler_params=pltpu.CompilerParams(vmem_limit_bytes=63 * 1024 * 1024),
        name="finish",
    )(fresh, outs)
    return new_down.T, new_up, decoded.reshape(residual.shape)


def solution(mesh):
    groups, shards = mesh.shape["group"], mesh.shape["shard"]
    nx, nz, ny = torus(shards)
    placed = (
        P("group", "shard", None),
        P("group", "shard", None),
        P("shard", None),
        P("shard", None),
        P("shard", None),
        P("group", None, None, "shard"),
        P("group", None, None, None),
    )

    def whole(learner_inputs, learner_cotangent, *others):
        tokens, width = learner_inputs.shape[1:]
        features = learner_cotangent.shape[2]
        rates = (
            0.5 * math.sqrt(RANK) / (SCALE * math.sqrt(width * features) * math.sqrt(tokens)),
            0.5 / (SCALE * math.sqrt(RANK) * math.sqrt(tokens)),
        )
        return jax.shard_map(
            functools.partial(per_device, (nx, nz, ny, groups), rates),
            mesh=mesh,
            in_specs=placed,
            out_specs=(P("shard", None), P("shard", None), P("group", None, None, None)),
            check_vma=False,
        )(learner_inputs, learner_cotangent, *others)

    return whole
```

```python
import functools
import math

import jax
import jax.numpy as jnp
from jax import lax
from jax.experimental import pallas as pl
from jax.experimental.pallas import tpu as pltpu
from jax.sharding import PartitionSpec as P

RANK = 64
SCALE = 2.0
F32 = jnp.float32
BF16 = jnp.bfloat16
NT = (((1,), (1,)), ((), ()))


def torus(shards):
    return {64: (4, 8, 2), 8: (2, 2, 2)}[shards]


def left_half(shape):
    return lax.broadcasted_iota(jnp.int32, shape, 1) < 64


def halves(even, odd):
    keep = left_half(even.shape)
    first = jnp.where(keep, even, pltpu.roll(odd, 64, 1))
    second = jnp.where(keep, pltpu.roll(even, 64, 1), odd)
    return first, second


def kernel(
    sizes, rates,
    x_hbm, c_hbm, down_hbm, up_hbm, w_hbm, ctx_hbm, res_hbm,
    new_hbm, out_hbm,
    x_v, c_v, down_v, up_v, w_v, ctx_v, res_v,
    up_all, down_all, up_flat, down_flat,
    gd, rd, sd, qd, gu, ru, su, qu,
    base, rb, sb, qb, fresh, tz, txy, outs,
    base_line, up_line, frozen, squares,
    local_sem, send_sem, recv_sem, ready_sem,
):
    nx, nz, ny, groups = sizes
    group = lax.axis_index("group")
    shard = lax.axis_index("shard")
    y = lax.rem(shard, ny)
    z = lax.rem(shard // ny, nz)
    x = shard // (ny * nz)
    other = 1 - y
    learner = group == 0
    helper_group = jnp.where(other == 1, groups - 2, 2)
    helper = group == jnp.where(y == 1, groups - 2, 2)

    def at(xx, zz, yy):
        return (xx * nz + zz) * ny + yy

    def x_to(d):
        return lax.rem(x + d, nx)

    def z_to(d):
        return lax.rem(z + d, nz)

    def y_to(d):
        return lax.rem(y + d, ny)

    def hops(d, n):
        return min(d, n - d)

    line = sorted(range(1, nz), key=lambda d: -hops(d, nz))
    rows = sorted(range(nx), key=lambda d: -hops(d, nx))
    plane = [(dx, dy) for dx in rows for dy in (1, 0) if (dx, dy) != (0, 0)]

    local = [
        pltpu.make_async_copy(src, dst, local_sem.at[i])
        for i, (src, dst) in enumerate(
            [
                (up_hbm, up_v),
                (down_hbm, down_v),
                (ctx_hbm, ctx_v),
                (w_hbm, w_v),
                (res_hbm.at[:, pl.ds(pl.multiple_of(x * (nz * 128), 128), nz * 128)], res_v),
                (c_hbm, c_v),
                (x_hbm, x_v),
            ]
        )
    ]
    barrier = pltpu.get_barrier_semaphore()
    peers = [at(x, z_to(d), y) for d in line] + [at(x_to(dx), z, y_to(dy)) for dx, dy in plane]
    for peer in peers:
        pl.semaphore_signal(
            barrier, inc=1, device_id={"shard": peer}, device_id_type=pl.DeviceIdType.MESH
        )

    @pl.when(learner)
    def _():
        for d in range(1, nx):
            pl.semaphore_signal(
                barrier, inc=1, device_id={"group": helper_group, "shard": at(x_to(d), z, other)},
                device_id_type=pl.DeviceIdType.MESH,
            )
        for g in range(1, groups):
            pl.semaphore_signal(
                barrier, inc=1, device_id={"group": g}, device_id_type=pl.DeviceIdType.MESH
            )

    for copy in local[:5]:
        copy.start()

    @pl.when(learner)
    def _():
        local[5].start()
        local[6].start()

    used = [0]

    def remote(src, dst, peer):
        k = used[0]
        used[0] += 1
        return pltpu.make_async_remote_copy(
            src_ref=src, dst_ref=dst, send_sem=send_sem.at[k], recv_sem=recv_sem.at[k],
            device_id={"shard": peer}, device_id_type=pl.DeviceIdType.MESH,
        )

    def along(ref_of, dst_of):
        return [remote(ref_of(z_to(d)), dst_of(i, d), at(x, z_to(d), y)) for i, d in enumerate(line)]

    def across(ref_of, dst_of):
        return [
            remote(ref_of(x_to(dx), y_to(dy)), dst_of(i), at(x_to(dx), z, y_to(dy)))
            for i, (dx, dy) in enumerate(plane)
        ]

    def beside(ref):
        return [remote(ref, ref, at(x_to(d), z, y)) for d in rows if d]

    def helped(ref):
        copies = []
        for d in rows[:-1]:
            k = used[0]
            used[0] += 1
            copies.append(
                pltpu.make_async_remote_copy(
                    src_ref=ref, dst_ref=ref, send_sem=send_sem.at[k], recv_sem=recv_sem.at[k],
                    device_id={"group": 0, "shard": at(x_to(d), z, other)},
                    device_id_type=pl.DeviceIdType.MESH,
                )
            )
        return copies

    def start(copies, started):
        for copy in copies:
            copy.start()
        started.extend(copies)

    def arrive(copies):
        for copy in copies:
            copy.wait_recv()

    def sent(started):
        for copy in started:
            copy.wait_send()

    learnt, lent, decoded = [], [], []

    up_z = along(lambda zz: up_all.at[y, x, z], lambda i, d: up_all.at[y, x, z])
    down_z = along(lambda zz: down_all.at[y, x, z], lambda i, d: down_all.at[y, x, z])
    up_x = beside(up_all.at[y, x])
    up_x += [remote(up_all.at[y, x], up_all.at[y, x], at(x, z, other))]
    up_y = helped(up_all.at[y, x])
    down_x = beside(down_all.at[y, x])
    down_p = [remote(down_all.at[y, x], down_all.at[y, x], at(x, z, other))]
    down_y = helped(down_all.at[y, x])
    gd_xy = across(lambda xx, yy: gd.at[yy, xx], lambda i: rd.at[i])
    gd_z = along(lambda zz: sd.at[zz], lambda i, d: qd.at[i])
    gu_xy = across(lambda xx, yy: gu.at[yy, xx], lambda i: ru.at[i])
    gu_z = along(lambda zz: su.at[zz], lambda i, d: qu.at[i])
    base_xy = across(lambda xx, yy: base.at[yy, xx], lambda i: rb.at[i])
    base_z = along(lambda zz: sb.at[zz], lambda i, d: qb.at[i])
    base_g = along(lambda zz: base_line.at[z], lambda i, d: base_line.at[z])
    up_g = along(lambda zz: up_line.at[z], lambda i, d: up_line.at[z])
    low_z = along(lambda zz: tz.at[0], lambda i, d: tz.at[i + 1])
    low_xy = across(lambda xx, yy: txy.at[0], lambda i: txy.at[i + 1])
    out_xy = across(lambda xx, yy: outs, lambda i: out_hbm.at[y, x])
    out_own = pltpu.make_async_copy(outs, out_hbm.at[y, x], local_sem.at[7])

    def spread(part, k):
        order = [g for hi in (2, 1, 3, 0) for g in (2 * hi, 2 * hi + 1) if 0 < g < groups]
        return [
            pltpu.make_async_remote_copy(
                src_ref=part, dst_ref=part, send_sem=send_sem.at[k + i], recv_sem=recv_sem.at[k],
                device_id={"group": g}, device_id_type=pl.DeviceIdType.MESH,
            )
            for i, g in enumerate(order)
        ]

    down_spread = spread(fresh, used[0])
    up_spread = spread(up_line.at[z], used[0] + groups - 1)

    def summed(own, others, index=()):
        total = own.astype(F32)
        for i in range(others.shape[0]):
            total = total + others[(i, *index)].astype(F32)
        return total

    def packed_up():
        up_t = up_v[...].T
        up_t = jnp.concatenate([up_t, jnp.zeros_like(up_t)], axis=1)
        return halves(up_t[0:32], up_t[32:64])[0]

    def project(xx, _):
        for zz in range(nz):
            column = pl.multiple_of((xx * nz + zz) * 128, 128)
            block = jnp.dot(ctx_v[...], w_v[:, pl.ds(column, 128)], preferred_element_type=F32)
            even, odd = halves(block[0:16], block[16:32])
            base[0, xx, zz] = even.astype(BF16)
            base[1, xx, zz] = odd.astype(BF16)
        return 0

    def base_lines():
        arrive(base_xy)
        for d, copy in zip(line, base_z):
            zz = z_to(d)
            sb[zz] = summed(base[y, x, zz], rb, (zz,)).astype(BF16)
            copy.start()
        sb[z] = summed(base[y, x, z], rb, (z,)).astype(BF16)

    def base_total():
        arrive(base_z)
        base_line[z] = summed(sb[z], qb).astype(BF16)
        start(base_g, [])

    def freeze():
        arrive(base_g)
        local[4].wait()
        for zz in range(nz):
            held = res_v[:, zz * 128 : (zz + 1) * 128].astype(F32)
            even, odd = halves(held[0:16], held[16:32])
            frozen[:, zz * 128 : (zz + 1) * 128] = base_line[zz].astype(F32) + jnp.where(
                y == 0, even, odd
            )

    local[0].wait()
    packed = packed_up()
    pl.semaphore_wait(
        barrier,
        len(peers) + jnp.where(learner, 0, 1) + jnp.where(helper, nx - 1, 0),
    )

    @pl.when(jnp.logical_not(learner))
    def _():
        pl.semaphore_signal(
            ready_sem, inc=1, device_id={"group": 0}, device_id_type=pl.DeviceIdType.MESH
        )

    local[1].wait()

    @pl.when(jnp.logical_or(learner, helper))
    def _():
        up_all[y, x, z] = packed.astype(BF16)
        for copy in up_z:
            copy.start()
        down_all[y, x, z] = down_v[...].astype(BF16)
        for copy in down_z:
            copy.start()
        arrive(up_z)

        @pl.when(learner)
        def _():
            start(up_x, learnt)

        @pl.when(helper)
        def _():
            start(up_y, lent)

        arrive(down_z)

        @pl.when(learner)
        def _():
            start(down_x + down_p, learnt)

        @pl.when(helper)
        def _():
            start(down_y, lent)

    learnt.extend(up_z + down_z)
    lent.extend(up_z + down_z)
    local[2].wait()
    local[3].wait()
    lax.fori_loop(0, nx, project, 0)

    @pl.when(jnp.logical_not(learner))
    def _():
        start(base_xy, [])
        base_lines()
        base_total()
        freeze()

    @pl.when(learner)
    def _():
        local[5].wait()
        arrive(up_x)
        arrive(up_y)

        def unpack_up(xx, _):
            for zz in range(nz):
                column = pl.multiple_of((xx * nz + zz) * 128, 128)
                top, low = halves(
                    up_all[0, xx, zz].astype(F32), up_all[1, xx, zz].astype(F32)
                )
                up_flat[:, pl.ds(column, 128)] = jnp.concatenate([top, low], axis=0).astype(BF16)
            return 0

        lax.fori_loop(0, nx, unpack_up, 0)
        lifted = lax.dot_general(
            up_flat[...], c_v[...], NT, preferred_element_type=F32
        ).astype(BF16)
        local[6].wait()
        for dx in rows:
            xx = x_to(dx)
            for zz in range(nz):
                column = pl.multiple_of((xx * nz + zz) * 256, 256)
                block = jnp.dot(lifted, x_v[:, pl.ds(column, 256)], preferred_element_type=F32)
                block = block.astype(BF16)
                gd[0, xx, zz] = block[:, 0:128]
                gd[1, xx, zz] = block[:, 128:256]
            start([c for c, p in zip(gd_xy, plane) if p[0] == dx], learnt)
        start(base_xy, [])
        def flatten(plane_y):
            for xx in range(nx):
                for zz in range(nz):
                    column = pl.multiple_of((xx * nz + zz) * 256 + plane_y * 128, 128)
                    down_flat[:, pl.ds(column, 128)] = down_all[plane_y, xx, zz]

        arrive(down_x)
        flatten(y)
        arrive(down_p)
        arrive(down_y)
        flatten(other)
        lowered = lax.dot_general(
            down_flat[...], x_v[...], NT, preferred_element_type=F32
        ).astype(BF16)
        for dx in rows:
            xx = x_to(dx)
            for zz in range(nz):
                column = pl.multiple_of((xx * nz + zz) * 128, 128)
                block = jnp.dot(lowered, c_v[:, pl.ds(column, 128)], preferred_element_type=F32)
                even, odd = halves(block[0:32], block[32:64])
                gu[0, xx, zz] = even.astype(BF16)
                gu[1, xx, zz] = odd.astype(BF16)
            start([c for c, p in zip(gu_xy, plane) if p[0] == dx], learnt)
        arrive(gd_xy)
        for d, copy in zip(line, gd_z):
            zz = z_to(d)
            sd[zz] = summed(gd[y, x, zz], rd, (zz,)).astype(BF16)
            start([copy], learnt)
        sd[z] = summed(gd[y, x, z], rd, (z,)).astype(BF16)
        base_lines()
        arrive(gd_z)
        total = summed(sd[z], qd)
        fresh[...] = (down_v[...] - rates[0] * (SCALE * total)).astype(BF16)
        pl.semaphore_wait(ready_sem, groups - 1)
        start(down_spread, learnt)
        arrive(gu_xy)
        for d, copy in zip(line, gu_z):
            zz = z_to(d)
            su[zz] = summed(gu[y, x, zz], ru, (zz,)).astype(BF16)
            start([copy], learnt)
        su[z] = summed(gu[y, x, z], ru, (z,)).astype(BF16)

    decoded.extend(base_xy + base_z + base_g)

    @pl.when(jnp.logical_not(learner))
    def _():
        down_spread[0].wait_recv()

    new_down = fresh[...]
    nothing = jnp.zeros_like(new_down)
    first = jnp.concatenate([new_down, nothing], axis=0)
    second = jnp.concatenate([nothing, new_down], axis=0)
    rows_low = lax.dot_general(
        ctx_v[0:16], first, NT, preferred_element_type=F32
    ) + lax.dot_general(ctx_v[16:32], second, NT, preferred_element_type=F32)
    tz[0] = rows_low.astype(BF16)
    start(low_z, decoded)

    @pl.when(learner)
    def _():
        base_total()
        arrive(gu_z)
        up_line[z] = (packed - rates[1] * (SCALE * summed(su[z], qu))).astype(BF16)
        start(up_spread, learnt)
        start(up_g, [])

    arrive(low_z)
    txy[0] = jnp.sum(tz[...].astype(F32), axis=0).astype(BF16)
    start(low_xy, decoded)

    @pl.when(learner)
    def _():
        freeze()

    @pl.when(jnp.logical_not(learner))
    def _():
        up_spread[0].wait_recv()
        start(up_g, [])

    written = [
        pltpu.make_async_copy(fresh, new_hbm.at[0:64], local_sem.at[8]),
        pltpu.make_async_copy(up_line.at[z], new_hbm.at[64:96], local_sem.at[9]),
    ]
    for copy in written:
        copy.start()
    sent([copy for copy in decoded if not any(copy is late for late in low_xy)])

    @pl.when(learner)
    def _():
        sent(learnt)

    @pl.when(helper)
    def _():
        sent(lent)

    arrive(up_g)
    for zz in range(nz):
        new_up = up_line[zz].astype(F32)
        turned = pltpu.roll(new_up, 64, 1)
        keep = left_half(new_up.shape)
        squares[:, zz * 128 : (zz + 1) * 128] = jnp.concatenate(
            [
                jnp.where(keep, new_up, 0.0),
                jnp.where(keep, turned, 0.0),
                jnp.where(keep, 0.0, turned),
                jnp.where(keep, 0.0, new_up),
            ],
            axis=0,
        ).astype(BF16)
    arrive(low_xy)
    lowered_rows = jnp.sum(txy[...].astype(F32), axis=0).astype(BF16)
    delta = jnp.dot(lowered_rows, squares[...], preferred_element_type=F32)
    for zz in range(nz):
        part = slice(zz * 128, (zz + 1) * 128)
        outs[zz] = (frozen[:, part] + SCALE * delta[:, part]).astype(BF16)
    start(out_xy, decoded)
    out_own.start()
    arrive(out_xy)

    out_own.wait()
    for copy in written:
        copy.wait()
    sent(up_g + low_xy + out_xy)


def finish(fresh_ref, outs_ref, down_ref, up_ref, dec_ref):
    ny, nx, nz = outs_ref.shape[:3]
    down_ref[...] = fresh_ref[0:64]
    packed = fresh_ref[64:96].astype(F32)
    up_t = jnp.concatenate([packed, pltpu.roll(packed, 64, 1)], axis=0)
    up_ref[...] = up_t.T[0:64].astype(BF16)
    for xx in range(nx):
        for zz in range(nz):
            column = (xx * nz + zz) * 128
            top, low = halves(outs_ref[0, xx, zz].astype(F32), outs_ref[1, xx, zz].astype(F32))
            dec_ref[0:16, column : column + 128] = top.astype(BF16)
            dec_ref[16:32, column : column + 128] = low.astype(BF16)


def per_device(
    sizes, rates,
    learner_inputs, learner_cotangent, down_factor, up_factor, weight, context, residual
):
    nx, nz, ny, groups = sizes
    tokens, width = learner_inputs.shape[1:]
    features = learner_cotangent.shape[2]
    rows = context.shape[1] * context.shape[2]
    xy = nx * ny - 1
    copies = 8 * (nz - 1) + 5 * xy + 2 * (2 * nx - 1) + 2 * (groups - 1)
    blocks = (ny, nx, nz)
    scratch = [
        pltpu.VMEM((tokens, width), BF16),
        pltpu.VMEM((tokens, features), BF16),
        pltpu.VMEM(down_factor.shape[::-1], F32),
        pltpu.VMEM(up_factor.shape, F32),
        pltpu.VMEM(weight.shape, BF16),
        pltpu.VMEM((rows, 128), BF16),
        pltpu.VMEM((rows, nz * 128), BF16),
        pltpu.VMEM((*blocks, 32, 128), BF16),
        pltpu.VMEM((*blocks, 64, 128), BF16),
        pltpu.VMEM((RANK, features), BF16),
        pltpu.VMEM((RANK, width), BF16),
    ]
    for height in (64, 32, 16):
        scratch += [
            pltpu.VMEM((*blocks, height, 128), BF16),
            pltpu.VMEM((xy, nz, height, 128), BF16),
            pltpu.VMEM((nz, height, 128), BF16),
            pltpu.VMEM((nz - 1, height, 128), BF16),
        ]
    scratch += [
        pltpu.VMEM((64, 128), BF16),
        pltpu.VMEM((nz, 16, 128), BF16),
        pltpu.VMEM((xy + 1, 16, 128), BF16),
        pltpu.VMEM((nz, 16, 128), BF16),
        pltpu.VMEM((nz, 16, 128), BF16),
        pltpu.VMEM((nz, 32, 128), BF16),
        pltpu.VMEM((16, nz * 128), F32),
        pltpu.VMEM((128, nz * 128), BF16),
        pltpu.SemaphoreType.DMA((10,)),
        pltpu.SemaphoreType.DMA((copies,)),
        pltpu.SemaphoreType.DMA((copies,)),
        pltpu.SemaphoreType.REGULAR,
    ]
    fresh, outs = pl.pallas_call(
        functools.partial(kernel, sizes, rates),
        out_shape=(
            jax.ShapeDtypeStruct((96, 128), BF16),
            jax.ShapeDtypeStruct((*blocks, 16, 128), BF16),
        ),
        in_specs=[pl.BlockSpec(memory_space=pltpu.HBM)] * 7,
        out_specs=(pl.BlockSpec(memory_space=pltpu.HBM),) * 2,
        scratch_shapes=scratch,
        compiler_params=pltpu.CompilerParams(
            collective_id=0, has_side_effects=True, vmem_limit_bytes=63 * 1024 * 1024
        ),
        name="lora_step",
    )(
        learner_inputs[0], learner_cotangent[0], down_factor.T, up_factor, weight,
        context[0].reshape(rows, -1), residual[0].reshape(rows, features),
    )
    new_down, new_up, decoded = pl.pallas_call(
        finish,
        out_shape=(
            jax.ShapeDtypeStruct((64, 128), BF16),
            jax.ShapeDtypeStruct((64, 64), BF16),
            jax.ShapeDtypeStruct((rows, features), BF16),
        ),
        in_specs=[pl.BlockSpec(memory_space=pltpu.VMEM)] * 2,
        out_specs=(pl.BlockSpec(memory_space=pltpu.VMEM),) * 3,
        compiler_params=pltpu.CompilerParams(vmem_limit_bytes=63 * 1024 * 1024),
        name="finish",
    )(fresh, outs)
    return new_down.T, new_up, decoded.reshape(residual.shape)


def solution(mesh):
    groups, shards = mesh.shape["group"], mesh.shape["shard"]
    nx, nz, ny = torus(shards)
    placed = (
        P("group", "shard", None),
        P("group", "shard", None),
        P("shard", None),
        P("shard", None),
        P("shard", None),
        P("group", None, None, "shard"),
        P("group", None, None, None),
    )

    def whole(learner_inputs, learner_cotangent, *others):
        tokens, width = learner_inputs.shape[1:]
        features = learner_cotangent.shape[2]
        rates = (
            0.5 * math.sqrt(RANK) / (SCALE * math.sqrt(width * features) * math.sqrt(tokens)),
            0.5 / (SCALE * math.sqrt(RANK) * math.sqrt(tokens)),
        )
        return jax.shard_map(
            functools.partial(per_device, (nx, nz, ny, groups), rates),
            mesh=mesh,
            in_specs=placed,
            out_specs=(P("shard", None), P("shard", None), P("group", None, None, None)),
            check_vma=False,
        )(learner_inputs, learner_cotangent, *others)

    return whole
```

```python
import functools
import math

import jax
import jax.numpy as jnp
from jax import lax
from jax.experimental import pallas as pl
from jax.experimental.pallas import tpu as pltpu
from jax.sharding import PartitionSpec as P

RANK = 64
SCALE = 2.0
F32 = jnp.float32
BF16 = jnp.bfloat16
NT = (((1,), (1,)), ((), ()))


def torus(shards):
    return {64: (4, 8, 2), 8: (2, 2, 2)}[shards]


def left_half(shape):
    return lax.broadcasted_iota(jnp.int32, shape, 1) < 64


def halves(even, odd):
    keep = left_half(even.shape)
    first = jnp.where(keep, even, pltpu.roll(odd, 64, 1))
    second = jnp.where(keep, pltpu.roll(even, 64, 1), odd)
    return first, second


def kernel(
    sizes, rates,
    x_hbm, c_hbm, down_hbm, up_hbm, w_hbm, ctx_hbm, res_hbm,
    new_hbm, out_hbm,
    x_v, c_v, down_v, up_v, w_v, ctx_v, res_v,
    up_all, down_all, up_flat, down_flat,
    gd, rd, sd, qd, gu, ru, su, qu,
    base, rb, sb, qb, fresh, tz, txy, outs,
    base_line, up_line, frozen, squares,
    local_sem, send_sem, recv_sem, ready_sem,
):
    nx, nz, ny, groups = sizes
    group = lax.axis_index("group")
    shard = lax.axis_index("shard")
    y = lax.rem(shard, ny)
    z = lax.rem(shard // ny, nz)
    x = shard // (ny * nz)
    other = 1 - y
    learner = group == 0
    helper_group = jnp.where(other == 1, groups - 2, 2)
    helper = group == jnp.where(y == 1, groups - 2, 2)

    def at(xx, zz, yy):
        return (xx * nz + zz) * ny + yy

    def x_to(d):
        return lax.rem(x + d, nx)

    def z_to(d):
        return lax.rem(z + d, nz)

    def y_to(d):
        return lax.rem(y + d, ny)

    def hops(d, n):
        return min(d, n - d)

    line = sorted(range(1, nz), key=lambda d: -hops(d, nz))
    rows = sorted(range(nx), key=lambda d: -hops(d, nx))
    plane = [(dx, dy) for dx in rows for dy in (1, 0) if (dx, dy) != (0, 0)]

    local = [
        pltpu.make_async_copy(src, dst, local_sem.at[i])
        for i, (src, dst) in enumerate(
            [
                (up_hbm, up_v),
                (down_hbm, down_v),
                (ctx_hbm, ctx_v),
                (w_hbm, w_v),
                (res_hbm.at[:, pl.ds(pl.multiple_of(x * (nz * 128), 128), nz * 128)], res_v),
                (c_hbm, c_v),
                (x_hbm, x_v),
            ]
        )
    ]
    barrier = pltpu.get_barrier_semaphore()
    peers = [at(x, z_to(d), y) for d in line] + [at(x_to(dx), z, y_to(dy)) for dx, dy in plane]
    for peer in peers:
        pl.semaphore_signal(
            barrier, inc=1, device_id={"shard": peer}, device_id_type=pl.DeviceIdType.MESH
        )

    @pl.when(learner)
    def _():
        for d in range(1, nx):
            pl.semaphore_signal(
                barrier, inc=1, device_id={"group": helper_group, "shard": at(x_to(d), z, other)},
                device_id_type=pl.DeviceIdType.MESH,
            )
        for g in range(1, groups):
            pl.semaphore_signal(
                barrier, inc=1, device_id={"group": g}, device_id_type=pl.DeviceIdType.MESH
            )

    for copy in local[:5]:
        copy.start()

    @pl.when(learner)
    def _():
        local[5].start()
        local[6].start()

    used = [0]

    def remote(src, dst, peer):
        k = used[0]
        used[0] += 1
        return pltpu.make_async_remote_copy(
            src_ref=src, dst_ref=dst, send_sem=send_sem.at[k], recv_sem=recv_sem.at[k],
            device_id={"shard": peer}, device_id_type=pl.DeviceIdType.MESH,
        )

    def along(ref_of, dst_of):
        return [remote(ref_of(z_to(d)), dst_of(i, d), at(x, z_to(d), y)) for i, d in enumerate(line)]

    def across(ref_of, dst_of):
        return [
            remote(ref_of(x_to(dx), y_to(dy)), dst_of(i), at(x_to(dx), z, y_to(dy)))
            for i, (dx, dy) in enumerate(plane)
        ]

    def beside(ref):
        return [remote(ref, ref, at(x_to(d), z, y)) for d in rows if d]

    def helped(ref):
        copies = []
        for d in rows[:-1]:
            k = used[0]
            used[0] += 1
            copies.append(
                pltpu.make_async_remote_copy(
                    src_ref=ref, dst_ref=ref, send_sem=send_sem.at[k], recv_sem=recv_sem.at[k],
                    device_id={"group": 0, "shard": at(x_to(d), z, other)},
                    device_id_type=pl.DeviceIdType.MESH,
                )
            )
        return copies

    def start(copies, started):
        for copy in copies:
            copy.start()
        started.extend(copies)

    def arrive(copies):
        for copy in copies:
            copy.wait_recv()

    def sent(started):
        for copy in started:
            copy.wait_send()

    learnt, lent, decoded = [], [], []

    up_z = along(lambda zz: up_all.at[y, x, z], lambda i, d: up_all.at[y, x, z])
    down_z = along(lambda zz: down_all.at[y, x, z], lambda i, d: down_all.at[y, x, z])
    up_x = beside(up_all.at[y, x])
    up_x += [remote(up_all.at[y, x], up_all.at[y, x], at(x, z, other))]
    up_y = helped(up_all.at[y, x])
    down_x = beside(down_all.at[y, x])
    down_p = [remote(down_all.at[y, x], down_all.at[y, x], at(x, z, other))]
    down_y = helped(down_all.at[y, x])
    gd_xy = across(lambda xx, yy: gd.at[yy, xx], lambda i: rd.at[i])
    gd_z = along(lambda zz: sd.at[zz], lambda i, d: qd.at[i])
    gu_xy = across(lambda xx, yy: gu.at[yy, xx], lambda i: ru.at[i])
    gu_z = along(lambda zz: su.at[zz], lambda i, d: qu.at[i])
    base_xy = across(lambda xx, yy: base.at[yy, xx], lambda i: rb.at[i])
    base_z = along(lambda zz: sb.at[zz], lambda i, d: qb.at[i])
    base_g = along(lambda zz: base_line.at[z], lambda i, d: base_line.at[z])
    up_g = along(lambda zz: up_line.at[z], lambda i, d: up_line.at[z])
    low_z = along(lambda zz: tz.at[0], lambda i, d: tz.at[i + 1])
    low_xy = across(lambda xx, yy: txy.at[0], lambda i: txy.at[i + 1])
    out_xy = across(lambda xx, yy: outs, lambda i: out_hbm.at[y, x])
    out_own = pltpu.make_async_copy(outs, out_hbm.at[y, x], local_sem.at[7])

    def spread(part, k):
        order = [g for hi in (2, 1, 3, 0) for g in (2 * hi, 2 * hi + 1) if 0 < g < groups]
        return [
            pltpu.make_async_remote_copy(
                src_ref=part, dst_ref=part, send_sem=send_sem.at[k + i], recv_sem=recv_sem.at[k],
                device_id={"group": g}, device_id_type=pl.DeviceIdType.MESH,
            )
            for i, g in enumerate(order)
        ]

    down_spread = spread(fresh, used[0])
    up_spread = spread(up_line.at[z], used[0] + groups - 1)

    def summed(own, others, index=()):
        total = own.astype(F32)
        for i in range(others.shape[0]):
            total = total + others[(i, *index)].astype(F32)
        return total

    def packed_up():
        up_t = up_v[...].T
        up_t = jnp.concatenate([up_t, jnp.zeros_like(up_t)], axis=1)
        return halves(up_t[0:32], up_t[32:64])[0]

    def project(xx, _):
        for zz in range(nz):
            column = pl.multiple_of((xx * nz + zz) * 128, 128)
            block = jnp.dot(ctx_v[...], w_v[:, pl.ds(column, 128)], preferred_element_type=F32)
            even, odd = halves(block[0:16], block[16:32])
            base[0, xx, zz] = even.astype(BF16)
            base[1, xx, zz] = odd.astype(BF16)
        return 0

    def base_lines():
        arrive(base_xy)
        for d, copy in zip(line, base_z):
            zz = z_to(d)
            sb[zz] = summed(base[y, x, zz], rb, (zz,)).astype(BF16)
            copy.start()
        sb[z] = summed(base[y, x, z], rb, (z,)).astype(BF16)

    def base_total():
        arrive(base_z)
        base_line[z] = summed(sb[z], qb).astype(BF16)
        start(base_g, [])

    def freeze():
        arrive(base_g)
        local[4].wait()
        for zz in range(nz):
            held = res_v[:, zz * 128 : (zz + 1) * 128].astype(F32)
            even, odd = halves(held[0:16], held[16:32])
            frozen[:, zz * 128 : (zz + 1) * 128] = base_line[zz].astype(F32) + jnp.where(
                y == 0, even, odd
            )

    local[0].wait()
    packed = packed_up()
    local[1].wait()
    up_all[y, x, z] = packed.astype(BF16)
    down_all[y, x, z] = down_v[...].astype(BF16)
    pl.semaphore_wait(
        barrier,
        len(peers) + jnp.where(learner, 0, 1) + jnp.where(helper, nx - 1, 0),
    )

    @pl.when(jnp.logical_not(learner))
    def _():
        pl.semaphore_signal(
            ready_sem, inc=1, device_id={"group": 0}, device_id_type=pl.DeviceIdType.MESH
        )

    @pl.when(jnp.logical_or(learner, helper))
    def _():
        for copy in up_z:
            copy.start()
        for copy in down_z:
            copy.start()
        arrive(up_z)

        @pl.when(learner)
        def _():
            start(up_x, learnt)

        @pl.when(helper)
        def _():
            start(up_y, lent)

        arrive(down_z)

        @pl.when(learner)
        def _():
            start(down_x + down_p, learnt)

        @pl.when(helper)
        def _():
            start(down_y, lent)

    learnt.extend(up_z + down_z)
    lent.extend(up_z + down_z)
    local[2].wait()
    local[3].wait()

    @pl.when(jnp.logical_not(learner))
    def _():
        lax.fori_loop(0, nx, project, 0)
        start(base_xy, [])
        base_lines()
        base_total()
        freeze()

    @pl.when(learner)
    def _():
        local[5].wait()
        arrive(up_x)
        arrive(up_y)

        def unpack_up(xx, _):
            for zz in range(nz):
                column = pl.multiple_of((xx * nz + zz) * 128, 128)
                top, low = halves(
                    up_all[0, xx, zz].astype(F32), up_all[1, xx, zz].astype(F32)
                )
                up_flat[:, pl.ds(column, 128)] = jnp.concatenate([top, low], axis=0).astype(BF16)
            return 0

        lax.fori_loop(0, nx, unpack_up, 0)
        lifted = lax.dot_general(
            up_flat[...], c_v[...], NT, preferred_element_type=F32
        ).astype(BF16)
        local[6].wait()
        for dx in rows:
            xx = x_to(dx)
            for zz in range(nz):
                column = pl.multiple_of((xx * nz + zz) * 256, 256)
                block = jnp.dot(lifted, x_v[:, pl.ds(column, 256)], preferred_element_type=F32)
                block = block.astype(BF16)
                gd[0, xx, zz] = block[:, 0:128]
                gd[1, xx, zz] = block[:, 128:256]
            start([c for c, p in zip(gd_xy, plane) if p[0] == dx], learnt)
        lax.fori_loop(0, nx, project, 0)
        start(base_xy, [])
        def flatten(plane_y):
            for xx in range(nx):
                for zz in range(nz):
                    column = pl.multiple_of((xx * nz + zz) * 256 + plane_y * 128, 128)
                    down_flat[:, pl.ds(column, 128)] = down_all[plane_y, xx, zz]

        arrive(down_x)
        flatten(y)
        arrive(down_p)
        arrive(down_y)
        flatten(other)
        lowered = lax.dot_general(
            down_flat[...], x_v[...], NT, preferred_element_type=F32
        ).astype(BF16)
        for dx in rows:
            xx = x_to(dx)
            for zz in range(nz):
                column = pl.multiple_of((xx * nz + zz) * 128, 128)
                block = jnp.dot(lowered, c_v[:, pl.ds(column, 128)], preferred_element_type=F32)
                even, odd = halves(block[0:32], block[32:64])
                gu[0, xx, zz] = even.astype(BF16)
                gu[1, xx, zz] = odd.astype(BF16)
            start([c for c, p in zip(gu_xy, plane) if p[0] == dx], learnt)
        arrive(gd_xy)
        for d, copy in zip(line, gd_z):
            zz = z_to(d)
            sd[zz] = summed(gd[y, x, zz], rd, (zz,)).astype(BF16)
            start([copy], learnt)
        sd[z] = summed(gd[y, x, z], rd, (z,)).astype(BF16)
        base_lines()
        arrive(gd_z)
        total = summed(sd[z], qd)
        fresh[...] = (down_v[...] - rates[0] * (SCALE * total)).astype(BF16)
        pl.semaphore_wait(ready_sem, groups - 1)
        start(down_spread, learnt)
        arrive(gu_xy)
        for d, copy in zip(line, gu_z):
            zz = z_to(d)
            su[zz] = summed(gu[y, x, zz], ru, (zz,)).astype(BF16)
            start([copy], learnt)
        su[z] = summed(gu[y, x, z], ru, (z,)).astype(BF16)

    decoded.extend(base_xy + base_z + base_g)

    @pl.when(jnp.logical_not(learner))
    def _():
        down_spread[0].wait_recv()

    new_down = fresh[...]
    nothing = jnp.zeros_like(new_down)
    first = jnp.concatenate([new_down, nothing], axis=0)
    second = jnp.concatenate([nothing, new_down], axis=0)
    rows_low = lax.dot_general(
        ctx_v[0:16], first, NT, preferred_element_type=F32
    ) + lax.dot_general(ctx_v[16:32], second, NT, preferred_element_type=F32)
    tz[0] = rows_low.astype(BF16)
    start(low_z, decoded)

    @pl.when(learner)
    def _():
        base_total()
        arrive(gu_z)
        up_line[z] = (packed - rates[1] * (SCALE * summed(su[z], qu))).astype(BF16)
        start(up_spread, learnt)
        start(up_g, [])

    @pl.when(jnp.logical_not(learner))
    def _():
        up_spread[0].wait_recv()
        start(up_g, [])

    arrive(low_z)
    txy[0] = jnp.sum(tz[...].astype(F32), axis=0).astype(BF16)
    start(low_xy, decoded)

    @pl.when(learner)
    def _():
        freeze()

    written = [
        pltpu.make_async_copy(fresh, new_hbm.at[0:64], local_sem.at[8]),
        pltpu.make_async_copy(up_line.at[z], new_hbm.at[64:96], local_sem.at[9]),
    ]
    for copy in written:
        copy.start()
    sent([copy for copy in decoded if not any(copy is late for late in low_xy)])

    @pl.when(learner)
    def _():
        sent(learnt)

    @pl.when(helper)
    def _():
        sent(lent)

    def square(zz):
        new_up = up_line[zz].astype(F32)
        turned = pltpu.roll(new_up, 64, 1)
        keep = left_half(new_up.shape)
        squares[:, pl.ds(pl.multiple_of(zz * 128, 128), 128)] = jnp.concatenate(
            [
                jnp.where(keep, new_up, 0.0),
                jnp.where(keep, turned, 0.0),
                jnp.where(keep, 0.0, turned),
                jnp.where(keep, 0.0, new_up),
            ],
            axis=0,
        ).astype(BF16)

    square(z)
    for d, copy in zip(line[::-1], up_g[::-1]):
        arrive([copy])
        square(lax.rem(z + nz - d, nz))
    arrive(low_xy)
    lowered_rows = jnp.sum(txy[...].astype(F32), axis=0).astype(BF16)
    delta = jnp.dot(lowered_rows, squares[...], preferred_element_type=F32)
    for zz in range(nz):
        part = slice(zz * 128, (zz + 1) * 128)
        outs[zz] = (frozen[:, part] + SCALE * delta[:, part]).astype(BF16)
    start(out_xy, decoded)
    out_own.start()
    arrive(out_xy)

    out_own.wait()
    for copy in written:
        copy.wait()
    sent(up_g + low_xy + out_xy)


def finish(fresh_ref, outs_ref, down_ref, up_ref, dec_ref):
    ny, nx, nz = outs_ref.shape[:3]
    down_ref[...] = fresh_ref[0:64]
    packed = fresh_ref[64:96].astype(F32)
    up_t = jnp.concatenate([packed, pltpu.roll(packed, 64, 1)], axis=0)
    up_ref[...] = up_t.T[0:64].astype(BF16)
    for xx in range(nx):
        for zz in range(nz):
            column = (xx * nz + zz) * 128
            top, low = halves(outs_ref[0, xx, zz].astype(F32), outs_ref[1, xx, zz].astype(F32))
            dec_ref[0:16, column : column + 128] = top.astype(BF16)
            dec_ref[16:32, column : column + 128] = low.astype(BF16)


def per_device(
    sizes, rates,
    learner_inputs, learner_cotangent, down_factor, up_factor, weight, context, residual
):
    nx, nz, ny, groups = sizes
    tokens, width = learner_inputs.shape[1:]
    features = learner_cotangent.shape[2]
    rows = context.shape[1] * context.shape[2]
    xy = nx * ny - 1
    copies = 8 * (nz - 1) + 5 * xy + 2 * (2 * nx - 1) + 2 * (groups - 1)
    blocks = (ny, nx, nz)
    scratch = [
        pltpu.VMEM((tokens, width), BF16),
        pltpu.VMEM((tokens, features), BF16),
        pltpu.VMEM(down_factor.shape[::-1], F32),
        pltpu.VMEM(up_factor.shape, F32),
        pltpu.VMEM(weight.shape, BF16),
        pltpu.VMEM((rows, 128), BF16),
        pltpu.VMEM((rows, nz * 128), BF16),
        pltpu.VMEM((*blocks, 32, 128), BF16),
        pltpu.VMEM((*blocks, 64, 128), BF16),
        pltpu.VMEM((RANK, features), BF16),
        pltpu.VMEM((RANK, width), BF16),
    ]
    for height in (64, 32, 16):
        scratch += [
            pltpu.VMEM((*blocks, height, 128), BF16),
            pltpu.VMEM((xy, nz, height, 128), BF16),
            pltpu.VMEM((nz, height, 128), BF16),
            pltpu.VMEM((nz - 1, height, 128), BF16),
        ]
    scratch += [
        pltpu.VMEM((64, 128), BF16),
        pltpu.VMEM((nz, 16, 128), BF16),
        pltpu.VMEM((xy + 1, 16, 128), BF16),
        pltpu.VMEM((nz, 16, 128), BF16),
        pltpu.VMEM((nz, 16, 128), BF16),
        pltpu.VMEM((nz, 32, 128), BF16),
        pltpu.VMEM((16, nz * 128), F32),
        pltpu.VMEM((128, nz * 128), BF16),
        pltpu.SemaphoreType.DMA((10,)),
        pltpu.SemaphoreType.DMA((copies,)),
        pltpu.SemaphoreType.DMA((copies,)),
        pltpu.SemaphoreType.REGULAR,
    ]
    fresh, outs = pl.pallas_call(
        functools.partial(kernel, sizes, rates),
        out_shape=(
            jax.ShapeDtypeStruct((96, 128), BF16),
            jax.ShapeDtypeStruct((*blocks, 16, 128), BF16),
        ),
        in_specs=[pl.BlockSpec(memory_space=pltpu.HBM)] * 7,
        out_specs=(pl.BlockSpec(memory_space=pltpu.HBM),) * 2,
        scratch_shapes=scratch,
        compiler_params=pltpu.CompilerParams(
            collective_id=0, has_side_effects=True, vmem_limit_bytes=63 * 1024 * 1024
        ),
        name="lora_step",
    )(
        learner_inputs[0], learner_cotangent[0], down_factor.T, up_factor, weight,
        context[0].reshape(rows, -1), residual[0].reshape(rows, features),
    )
    new_down, new_up, decoded = pl.pallas_call(
        finish,
        out_shape=(
            jax.ShapeDtypeStruct((64, 128), BF16),
            jax.ShapeDtypeStruct((64, 64), BF16),
            jax.ShapeDtypeStruct((rows, features), BF16),
        ),
        in_specs=[pl.BlockSpec(memory_space=pltpu.VMEM)] * 2,
        out_specs=(pl.BlockSpec(memory_space=pltpu.VMEM),) * 3,
        compiler_params=pltpu.CompilerParams(vmem_limit_bytes=63 * 1024 * 1024),
        name="finish",
    )(fresh, outs)
    return new_down.T, new_up, decoded.reshape(residual.shape)


def solution(mesh):
    groups, shards = mesh.shape["group"], mesh.shape["shard"]
    nx, nz, ny = torus(shards)
    placed = (
        P("group", "shard", None),
        P("group", "shard", None),
        P("shard", None),
        P("shard", None),
        P("shard", None),
        P("group", None, None, "shard"),
        P("group", None, None, None),
    )

    def whole(learner_inputs, learner_cotangent, *others):
        tokens, width = learner_inputs.shape[1:]
        features = learner_cotangent.shape[2]
        rates = (
            0.5 * math.sqrt(RANK) / (SCALE * math.sqrt(width * features) * math.sqrt(tokens)),
            0.5 / (SCALE * math.sqrt(RANK) * math.sqrt(tokens)),
        )
        return jax.shard_map(
            functools.partial(per_device, (nx, nz, ny, groups), rates),
            mesh=mesh,
            in_specs=placed,
            out_specs=(P("shard", None), P("shard", None), P("group", None, None, None)),
            check_vma=False,
        )(learner_inputs, learner_cotangent, *others)

    return whole
```
